32 devices in a mesh: hid: 8 (over z, y), wid: 4 (over x, core).
Axes of the slice: x: 2, y: 2, z: 4, core: 2. Of those that a mesh axis runs over, the one named last changes fastest.
Arguments:
- inputs: bfloat16 [512, 6144], P('hid', 'wid'), may hold values from -420 to 420
- cotangent: bfloat16 [512, 6144], P('hid', 'wid'), may hold values from -6 to 6
- norm_gain: float32 [6144], P('wid'), may hold values from 0.5 to 1.5
- qkv_weight: bfloat16 [6144, 3, 4096], P('wid', None, 'hid'), may hold values from -0.078125 to 0.078125
- out_weight: bfloat16 [4096, 6144], P('hid', 'wid'), may hold values from -0.375 to 0.375
- up_weight: bfloat16 [6144, 16384], P('wid', 'hid'), may hold values from -0.078125 to 0.078125
- down_weight: bfloat16 [16384, 6144], P('hid', 'wid'), may hold values from -0.046875 to 0.046875
- query_gain: float32 [128], replicated, may hold values from 0.5 to 1.5
- key_gain: float32 [128], replicated, may hold values from 0.5 to 1.5
Outputs:
- input_grad: bfloat16 [512, 6144], P('hid', 'wid')
- qkv_grad: bfloat16 [6144, 3, 4096], P('wid', None, 'hid')
- out_grad: bfloat16 [4096, 6144], P('hid', 'wid')
- up_grad: bfloat16 [6144, 16384], P('wid', 'hid')
- down_grad: bfloat16 [16384, 6144], P('hid', 'wid')
The draws below stay inside these ranges and needn't reach their ends.
All inputs are finite; a program needn't handle non-finite values.
Results may differ from the reference program's by a relative error of at most 0.011.
Values may be sent and summed in bfloat16 or wider, within the bound.
A program may use at most 128 MiB of HBM per device.

```python
import math
import jax
import jax.numpy as jnp
from jax import lax

D = 6144
FF = 16384
HEADS = 32
HEAD_DIM = 128
PATCHES = 256
TOKENS = 512


def draw_inputs(key, part):
    key = jax.random.fold_in(key, 11)
    column_key, row_key, base_key = jax.random.split(key, 3)
    rise = math.log10(3.0)
    column_ramp = jnp.arange(D, dtype=jnp.float32) / (D - 1) * rise
    column_scale = 10.0 ** (jax.random.uniform(column_key, (D,), jnp.float32) * (1.0 - rise) + column_ramp)
    row_scale = 10.0 ** jax.random.uniform(row_key, (TOKENS, 1), jnp.float32)
    base_values = jnp.clip(jax.random.normal(base_key, (TOKENS, D), jnp.float32), -4.0, 4.0)
    values = row_scale * column_scale * base_values
    return values.astype(jnp.bfloat16)


def level_of(stream_key, dims, cuts, smallest, high):
    def one(axis_at, blocks):
        draws = jax.random.uniform(jax.random.fold_in(jax.random.fold_in(stream_key, 6), axis_at), (blocks,), jnp.float32, smallest / len(cuts), high / len(cuts))
        return jnp.repeat(jnp.exp(draws), dims[axis_at] // blocks).reshape((-1,) + (1,) * (len(dims) - axis_at - 1))

    level = one(*cuts[0])
    for cut in cuts[1:]:
        level = level * one(*cut)
    return level


def bell_draw(own_key, extent, spread, limit, pieces=(), kind=jnp.bfloat16):
    array = jax.random.normal(own_key, extent, jnp.float32) * spread
    if len(pieces) > 0:
        array = level_of(own_key, extent, pieces, -0.22, 0.18) * array
    return jnp.clip(array, min=-limit, max=limit).astype(kind)


def setup_inputs(seed: int = 0) -> dict:
    keys = jax.random.split(jax.random.key(seed), 10)
    return {
        "inputs": draw_inputs(jax.random.fold_in(keys[9], 71), 0),
        "cotangent": bell_draw(keys[1], (TOKENS, D), 1.0, 6.0, ((0, 8), (1, 4))),
        "norm_gain": jnp.clip(1.0 + 0.1 * jax.random.normal(keys[2], (D,), jnp.float32), 0.5, 1.5),
        "qkv_weight": bell_draw(keys[3], (D, 3, HEADS * HEAD_DIM), D ** -0.5, 0.078125, ((0, 4), (2, 8))),
        "out_weight": bell_draw(keys[4], (HEADS * HEAD_DIM, D), (HEADS * HEAD_DIM // 16) ** -0.5, 0.375, ((0, 8), (1, 4))),
        "up_weight": bell_draw(keys[5], (D, FF), D ** -0.5, 0.078125, ((0, 4), (1, 8))),
        "down_weight": bell_draw(keys[6], (FF, D), FF ** -0.5, 0.046875, ((0, 8), (1, 4))),
        "query_gain": jnp.clip(1.0 + 0.1 * jax.random.normal(keys[7], (HEAD_DIM,), jnp.float32), 0.5, 1.5),
        "key_gain": jnp.clip(1.0 + 0.1 * jax.random.normal(keys[8], (HEAD_DIM,), jnp.float32), 0.5, 1.5),
    }


EPSILON = 1e-06

def product(form, left_arr, right_arr):
    return jnp.einsum(form, left_arr.astype(jnp.float32), right_arr.astype(jnp.float32))

def head_norm(values, gain):
    centre = lax.optimization_barrier(jnp.mean(values, axis=-1, keepdims=True))
    centred = values - centre
    inverse = lax.rsqrt(lax.optimization_barrier(jnp.mean(centred * centred, axis=-1, keepdims=True)) + EPSILON)
    unit_rows = centred * inverse
    return (unit_rows, inverse, unit_rows * gain)

def head_norm_back(upstream, unit_rows, inverse, gain):
    scaled = upstream * gain
    return inverse * (scaled - lax.optimization_barrier(jnp.mean(scaled, axis=-1, keepdims=True)) - unit_rows * lax.optimization_barrier(jnp.mean(scaled * unit_rows, axis=-1, keepdims=True)))

def gelu_pair(pre_act, upstream):
    hidden, pullback = jax.vjp(jax.nn.gelu, pre_act)
    return (hidden.astype(jnp.bfloat16), pullback(upstream)[0].astype(jnp.bfloat16))

def attention_pair(qkv_rows, att_grad, query_gain, key_gain):
    tok_count = qkv_rows.shape[0]
    head_width = qkv_rows.shape[2]
    head_count = head_width // HEAD_DIM
    image_count = tok_count // PATCHES
    score_scale = 1.0 / math.sqrt(HEAD_DIM)

    def per_image(values):
        return values.reshape(image_count, PATCHES, head_count, HEAD_DIM)
    query_unit, query_inverse, query_normed = head_norm(per_image(qkv_rows[:, 0]), query_gain)
    key_unit, key_inverse, key_normed = head_norm(per_image(qkv_rows[:, 1]), key_gain)
    query_normed = query_normed.astype(jnp.bfloat16)
    key_normed = key_normed.astype(jnp.bfloat16)
    value_rows = per_image(qkv_rows[:, 2]).astype(jnp.bfloat16)
    scores = product('ipha,iqha->ihpq', query_normed, key_normed) * score_scale
    exponent = jnp.exp(scores)
    probs = exponent / lax.optimization_barrier(jnp.sum(exponent, axis=-1, keepdims=True))
    probs_low = probs.astype(jnp.bfloat16)
    attended = product('ihpq,iqha->ipha', probs_low, value_rows).astype(jnp.bfloat16).reshape(tok_count, head_width)
    grad_rows = per_image(att_grad)
    probs_grad = product('ipha,iqha->ihpq', grad_rows, value_rows)
    value_grad = product('ihpq,ipha->iqha', probs_low, grad_rows)
    score_grad = (probs * (probs_grad - lax.optimization_barrier(jnp.sum(probs * probs_grad, axis=-1, keepdims=True))) * score_scale).astype(jnp.bfloat16)
    qn_grad = product('ihpq,iqha->ipha', score_grad, key_normed)
    kn_grad = product('ihpq,ipha->iqha', score_grad, query_normed)
    query_grad = head_norm_back(qn_grad, query_unit, query_inverse, query_gain)
    key_grad = head_norm_back(kn_grad, key_unit, key_inverse, key_gain)
    qkv_back = jnp.stack([query_grad.reshape(tok_count, head_width), key_grad.reshape(tok_count, head_width), value_grad.reshape(tok_count, head_width)], axis=1).astype(jnp.bfloat16)
    return (attended, qkv_back)

def reference(inputs, cotangent, norm_gain, qkv_weight, out_weight, up_weight, down_weight, query_gain, key_gain):
    input_rows = inputs.astype(jnp.float32)
    centre = lax.optimization_barrier(jnp.mean(input_rows, axis=-1, keepdims=True))
    centred = input_rows - centre
    inverse = lax.rsqrt(lax.optimization_barrier(jnp.mean(centred * centred, axis=-1, keepdims=True)) + EPSILON)
    unit_rows = centred * inverse
    normed = (unit_rows * norm_gain).astype(jnp.bfloat16)
    pre_act = jnp.dot(normed, up_weight, preferred_element_type=jnp.float32)
    qkv_rows = product('td,dch->tch', normed, qkv_weight)
    hidden_grad = jnp.dot(cotangent, down_weight.T, preferred_element_type=jnp.float32)
    att_grad = jnp.dot(cotangent, out_weight.T, preferred_element_type=jnp.float32).astype(jnp.bfloat16)
    hidden, pre_grad = gelu_pair(pre_act, hidden_grad)
    attended, qkv_back = attention_pair(qkv_rows, att_grad, query_gain, key_gain)
    qkv_grad = product('td,tch->dch', normed, qkv_back).astype(jnp.bfloat16)
    out_grad = jnp.dot(attended.T, cotangent, preferred_element_type=jnp.float32).astype(jnp.bfloat16)
    up_grad = jnp.dot(normed.T, pre_grad, preferred_element_type=jnp.float32).astype(jnp.bfloat16)
    down_grad = jnp.dot(hidden.T, cotangent, preferred_element_type=jnp.float32).astype(jnp.bfloat16)
    normed_grad = jnp.dot(pre_grad, up_weight.T, preferred_element_type=jnp.float32) + product('tch,dch->td', qkv_back, qkv_weight)
    unit_grad = normed_grad * norm_gain
    input_grad = (inverse * (unit_grad - lax.optimization_barrier(jnp.mean(unit_grad, axis=-1, keepdims=True)) - unit_rows * lax.optimization_barrier(jnp.mean(unit_grad * unit_rows, axis=-1, keepdims=True)))).astype(jnp.bfloat16)
    return (input_grad, qkv_grad, out_grad, up_grad, down_grad)
```

```python
import math

import jax
import jax.numpy as jnp
from jax import lax
from jax.sharding import PartitionSpec as P

HEAD_DIM = 128
PATCHES = 256


EPSILON = 1e-06


def swapped(value, axis, bit):
    size = lax.axis_size(axis)
    return lax.ppermute(value, axis, [(at, at ^ bit) for at in range(size)])


def axis_bits(axis):
    size = lax.axis_size(axis)
    return [1 << at for at in range(size.bit_length() - 1)]


def product(form, left_arr, right_arr):
    return jnp.einsum(form, left_arr, right_arr, preferred_element_type=jnp.float32)


def head_norm(values, gain):
    centre = jnp.mean(values, axis=-1, keepdims=True)
    centred = values - centre
    inverse = lax.rsqrt(jnp.mean(centred * centred, axis=-1, keepdims=True) + EPSILON)
    unit_rows = centred * inverse
    return (unit_rows, inverse, unit_rows * gain)


def head_norm_back(upstream, unit_rows, inverse, gain):
    scaled = upstream * gain
    return inverse * (
        scaled
        - jnp.mean(scaled, axis=-1, keepdims=True)
        - unit_rows * jnp.mean(scaled * unit_rows, axis=-1, keepdims=True)
    )


def gelu_pair(pre_act, upstream):
    hidden, pullback = jax.vjp(jax.nn.gelu, pre_act)
    return (hidden.astype(jnp.bfloat16), pullback(upstream)[0].astype(jnp.bfloat16))


def attention_pair(qkv_rows, att_grad, query_gain, key_gain):
    tok_count = qkv_rows.shape[0]
    head_width = qkv_rows.shape[2]
    head_count = head_width // HEAD_DIM
    image_count = tok_count // PATCHES
    score_scale = 1.0 / math.sqrt(HEAD_DIM)

    def per_image(values):
        return values.reshape(image_count, PATCHES, head_count, HEAD_DIM)

    query_unit, query_inverse, query_normed = head_norm(per_image(qkv_rows[:, 0]), query_gain)
    key_unit, key_inverse, key_normed = head_norm(per_image(qkv_rows[:, 1]), key_gain)
    query_normed = query_normed.astype(jnp.bfloat16)
    key_normed = key_normed.astype(jnp.bfloat16)
    value_rows = per_image(qkv_rows[:, 2]).astype(jnp.bfloat16)
    scores = product("ipha,iqha->ihpq", query_normed, key_normed) * score_scale
    exponent = jnp.exp(scores)
    probs = exponent / jnp.sum(exponent, axis=-1, keepdims=True)
    probs_low = probs.astype(jnp.bfloat16)
    attended = (
        product("ihpq,iqha->ipha", probs_low, value_rows)
        .astype(jnp.bfloat16)
        .reshape(tok_count, head_width)
    )
    grad_rows = per_image(att_grad)
    probs_grad = product("ipha,iqha->ihpq", grad_rows, value_rows)
    value_grad = product("ihpq,ipha->iqha", probs_low, grad_rows)
    score_grad = (
        probs * (probs_grad - jnp.sum(probs * probs_grad, axis=-1, keepdims=True)) * score_scale
    ).astype(jnp.bfloat16)
    qn_grad = product("ihpq,iqha->ipha", score_grad, key_normed)
    kn_grad = product("ihpq,ipha->iqha", score_grad, query_normed)
    query_grad = head_norm_back(qn_grad, query_unit, query_inverse, query_gain)
    key_grad = head_norm_back(kn_grad, key_unit, key_inverse, key_gain)
    qkv_back = jnp.stack(
        [
            query_grad.reshape(tok_count, head_width),
            key_grad.reshape(tok_count, head_width),
            value_grad.reshape(tok_count, head_width),
        ],
        axis=1,
    ).astype(jnp.bfloat16)
    return (attended, qkv_back)


def row_moments(input_rows):
    count = float(input_rows.shape[1])
    mean = jnp.mean(input_rows, axis=-1)
    deviation = input_rows - mean[:, None]
    square = jnp.sum(deviation * deviation, axis=-1)
    for bit in axis_bits("wid"):
        other_mean, other_square = swapped(jnp.stack([mean, square]), "wid", bit)
        offset = other_mean - mean
        mean = 0.5 * (mean + other_mean)
        square = square + other_square + offset * offset * (0.5 * count)
        count = 2.0 * count
    return (mean, lax.rsqrt(square / count + EPSILON), count)


def row_totals(sums):
    for bit in axis_bits("wid"):
        sums = sums + swapped(sums, "wid", bit)
    return sums


def halves(values, core):
    half = values.shape[0] // 2
    own = lax.dynamic_slice_in_dim(values, core * half, half, axis=0)
    other = lax.dynamic_slice_in_dim(values, (1 - core) * half, half, axis=0)
    return (own, other)


def summed_product(form, rows, weight):
    own, other = rows
    subtotal = product(form, own, weight) + swapped(
        product(form, other, weight).astype(jnp.bfloat16), "wid", 1
    ).astype(jnp.float32)
    for bit in axis_bits("wid")[1:]:
        subtotal = subtotal + swapped(
            subtotal.astype(jnp.bfloat16), "wid", bit
        ).astype(jnp.float32)
    return subtotal


def both_halves(own):
    return jnp.concatenate([own, swapped(own, "wid", 1)], axis=0)


CHUNKS = 4


def local(
    inputs,
    cotangent,
    norm_gain,
    qkv_weight,
    out_weight,
    up_weight,
    down_weight,
    query_gain,
    key_gain,
):
    core = lax.axis_index("wid") % 2
    grad_all = lax.all_gather(cotangent, "hid", axis=0, tiled=True)
    input_rows = inputs.astype(jnp.float32)
    centre, inverse, total_count = row_moments(input_rows)
    inverse = inverse[:, None]
    unit_rows = (input_rows - centre[:, None]) * inverse
    normed = (unit_rows * norm_gain).astype(jnp.bfloat16)
    normed_all = lax.all_gather(normed, "hid", axis=0, tiled=True)
    grad_halves = halves(grad_all, core)
    normed_halves = halves(normed_all, core)
    grad_order = jnp.concatenate(grad_halves, axis=0)
    normed_order = jnp.concatenate(normed_halves, axis=0)

    att_grad = summed_product("td,hd->th", grad_halves, out_weight).astype(jnp.bfloat16)
    width = up_weight.shape[1] // CHUNKS
    spans = [slice(at * width, (at + 1) * width) for at in range(CHUNKS)]
    hidden_grads = [
        summed_product("td,fd->tf", grad_halves, down_weight[span]) for span in spans
    ]
    qkv_rows = summed_product("td,dch->tch", normed_halves, qkv_weight)
    attended, qkv_back = attention_pair(qkv_rows, att_grad, query_gain, key_gain)
    attended = both_halves(attended)
    qkv_back = both_halves(qkv_back)
    normed_grad = product("tch,dch->td", qkv_back, qkv_weight)
    hidden, pre_grad = [], []
    for span, hidden_grad in zip(spans, hidden_grads):
        pre_act = summed_product("td,df->tf", normed_halves, up_weight[:, span])
        hidden_own, pre_own = gelu_pair(pre_act, hidden_grad)
        pre_both = both_halves(pre_own)
        pre_grad.append(pre_both)
        hidden.append(both_halves(hidden_own))
        normed_grad = normed_grad + product("tf,df->td", pre_both, up_weight[:, span])
    hidden = jnp.concatenate(hidden, axis=1)
    pre_grad = jnp.concatenate(pre_grad, axis=1)
    normed_grad = jnp.concatenate(halves(normed_grad, core), axis=0).astype(jnp.bfloat16)
    normed_grad = lax.psum_scatter(normed_grad, "hid", scatter_dimension=0, tiled=True)
    qkv_grad = product("td,tch->dch", normed_order, qkv_back).astype(jnp.bfloat16)
    out_grad = product("th,td->hd", attended, grad_order).astype(jnp.bfloat16)
    up_grad = product("td,tf->df", normed_order, pre_grad).astype(jnp.bfloat16)
    down_grad = product("tf,td->fd", hidden, grad_order).astype(jnp.bfloat16)
    unit_grad = normed_grad.astype(jnp.float32) * norm_gain
    grad_total, grad_project = row_totals(
        jnp.stack([jnp.sum(unit_grad, axis=-1), jnp.sum(unit_grad * unit_rows, axis=-1)])
    )
    input_grad = (
        inverse
        * (
            unit_grad
            - (grad_total / total_count)[:, None]
            - unit_rows * (grad_project / total_count)[:, None]
        )
    ).astype(jnp.bfloat16)
    return (input_grad, qkv_grad, out_grad, up_grad, down_grad)


def solution(mesh):
    placed = (
        P("hid", "wid"),
        P("hid", "wid"),
        P("wid"),
        P("wid", None, "hid"),
        P("hid", "wid"),
        P("wid", "hid"),
        P("hid", "wid"),
        P(),
        P(),
    )
    return jax.shard_map(
        local,
        mesh=mesh,
        in_specs=placed,
        out_specs=(
            P("hid", "wid"),
            P("wid", None, "hid"),
            P("hid", "wid"),
            P("wid", "hid"),
            P("hid", "wid"),
        ),
        check_vma=False,
    )
```

```python
import functools
import math

import jax
import jax.numpy as jnp
from jax import lax
from jax.experimental import pallas as pl
from jax.experimental.pallas import tpu as pltpu
from jax.sharding import PartitionSpec as P

HEAD_DIM = 128
PATCHES = 256


EPSILON = 1e-06


def swapped(value, axis, bit):
    size = lax.axis_size(axis)
    return lax.ppermute(value, axis, [(at, at ^ bit) for at in range(size)])


def axis_bits(axis):
    size = lax.axis_size(axis)
    return [1 << at for at in range(size.bit_length() - 1)]


def product(form, left_arr, right_arr):
    return jnp.einsum(form, left_arr, right_arr, preferred_element_type=jnp.float32)


def head_norm(values, gain):
    centre = jnp.mean(values, axis=-1, keepdims=True)
    centred = values - centre
    inverse = lax.rsqrt(jnp.mean(centred * centred, axis=-1, keepdims=True) + EPSILON)
    unit_rows = centred * inverse
    return (unit_rows, inverse, unit_rows * gain)


def head_norm_back(upstream, unit_rows, inverse, gain):
    scaled = upstream * gain
    return inverse * (
        scaled
        - jnp.mean(scaled, axis=-1, keepdims=True)
        - unit_rows * jnp.mean(scaled * unit_rows, axis=-1, keepdims=True)
    )


def gelu_pair(pre_act, upstream):
    hidden, pullback = jax.vjp(jax.nn.gelu, pre_act)
    return (hidden.astype(jnp.bfloat16), pullback(upstream)[0].astype(jnp.bfloat16))


def attention_pair(qkv_rows, att_grad, query_gain, key_gain):
    tok_count = qkv_rows.shape[0]
    head_width = qkv_rows.shape[2]
    head_count = head_width // HEAD_DIM
    image_count = tok_count // PATCHES
    score_scale = 1.0 / math.sqrt(HEAD_DIM)

    def per_image(values):
        return values.reshape(image_count, PATCHES, head_count, HEAD_DIM)

    query_unit, query_inverse, query_normed = head_norm(per_image(qkv_rows[:, 0]), query_gain)
    key_unit, key_inverse, key_normed = head_norm(per_image(qkv_rows[:, 1]), key_gain)
    query_normed = query_normed.astype(jnp.bfloat16)
    key_normed = key_normed.astype(jnp.bfloat16)
    value_rows = per_image(qkv_rows[:, 2]).astype(jnp.bfloat16)
    scores = product("ipha,iqha->ihpq", query_normed, key_normed) * score_scale
    exponent = jnp.exp(scores)
    probs = exponent / jnp.sum(exponent, axis=-1, keepdims=True)
    probs_low = probs.astype(jnp.bfloat16)
    attended = (
        product("ihpq,iqha->ipha", probs_low, value_rows)
        .astype(jnp.bfloat16)
        .reshape(tok_count, head_width)
    )
    grad_rows = per_image(att_grad)
    probs_grad = product("ipha,iqha->ihpq", grad_rows, value_rows)
    value_grad = product("ihpq,ipha->iqha", probs_low, grad_rows)
    score_grad = (
        probs * (probs_grad - jnp.sum(probs * probs_grad, axis=-1, keepdims=True)) * score_scale
    ).astype(jnp.bfloat16)
    qn_grad = product("ihpq,iqha->ipha", score_grad, key_normed)
    kn_grad = product("ihpq,ipha->iqha", score_grad, query_normed)
    query_grad = head_norm_back(qn_grad, query_unit, query_inverse, query_gain)
    key_grad = head_norm_back(kn_grad, key_unit, key_inverse, key_gain)
    qkv_back = jnp.stack(
        [
            query_grad.reshape(tok_count, head_width),
            key_grad.reshape(tok_count, head_width),
            value_grad.reshape(tok_count, head_width),
        ],
        axis=1,
    ).astype(jnp.bfloat16)
    return (attended, qkv_back)


def row_moments(input_rows):
    count = float(input_rows.shape[1])
    mean = jnp.mean(input_rows, axis=-1)
    deviation = input_rows - mean[:, None]
    square = jnp.sum(deviation * deviation, axis=-1)
    for bit in axis_bits("wid"):
        other_mean, other_square = swapped(jnp.stack([mean, square]), "wid", bit)
        offset = other_mean - mean
        mean = 0.5 * (mean + other_mean)
        square = square + other_square + offset * offset * (0.5 * count)
        count = 2.0 * count
    return (mean, lax.rsqrt(square / count + EPSILON), count)


def row_totals(sums):
    for bit in axis_bits("wid"):
        sums = sums + swapped(sums, "wid", bit)
    return sums


def halves(values, core):
    half = values.shape[0] // 2
    own = lax.dynamic_slice_in_dim(values, core * half, half, axis=0)
    other = lax.dynamic_slice_in_dim(values, (1 - core) * half, half, axis=0)
    return (own, other)


MESH = pl.DeviceIdType.MESH
CHUNK = 512


def forward_kernel(
    sizes,
    cot_ref,
    normed_ref,
    out_ref,
    down_ref,
    qkv_ref,
    up_ref,
    cot_all,
    normed_all,
    total,
    out_w,
    down_w,
    qkv_w,
    up_w,
    core_send,
    core_recv,
    x_send,
    x_recv,
    load_sem,
    slot_sem,
    rise_sem,
    fall_sem,
    pair_sem,
    core_out_sem,
    core_in_sem,
    x_out_sem,
    x_in_sem,
):
    depth, out_n, down_n, up_n, width = sizes
    hid, wid = lax.axis_index("hid"), lax.axis_index("wid")
    z, y = hid // 2, hid % 2
    core = wid % 2
    above, below, pair = hid + 2, hid - 2, z * 2 + 1 - y
    core_peer = wid + 1 - 2 * core
    x_peer = wid + 2 - 4 * ((wid // 2) % 2)

    loads = [
        pltpu.make_async_copy(src, dst, load_sem.at[at])
        for at, (src, dst) in enumerate(
            [(out_ref, out_w), (down_ref, down_w), (qkv_ref, qkv_w), (up_ref, up_w)]
        )
    ]
    for load in loads:
        load.start()

    gathered = (cot_all, normed_all)
    cot_all[hid] = cot_ref[...]
    normed_all[hid] = normed_ref[...]

    barrier = pltpu.get_barrier_semaphore()
    pl.semaphore_signal(barrier, inc=1, device_id={"hid": pair}, device_id_type=MESH)
    pl.semaphore_signal(barrier, inc=1, device_id={"wid": core_peer}, device_id_type=MESH)
    pl.semaphore_signal(barrier, inc=1, device_id={"wid": x_peer}, device_id_type=MESH)

    @pl.when(z < depth - 1)
    def _():
        pl.semaphore_signal(barrier, inc=1, device_id={"hid": above}, device_id_type=MESH)

    @pl.when(z > 0)
    def _():
        pl.semaphore_signal(barrier, inc=1, device_id={"hid": below}, device_id_type=MESH)

    neighbours = 3 + jnp.where(z > 0, 1, 0) + jnp.where(z < depth - 1, 1, 0)
    pl.semaphore_wait(barrier, neighbours)

    def block_copy(kind, level, side, sems, target):
        slot = level * 2 + side
        return pltpu.make_async_remote_copy(
            src_ref=gathered[kind].at[slot],
            dst_ref=gathered[kind].at[slot],
            send_sem=sems.at[kind, level],
            recv_sem=slot_sem.at[kind, slot],
            device_id={"hid": target},
            device_id_type=MESH,
        )

    def to_pair(kind, level):
        return block_copy(kind, level, y, pair_sem, pair)

    def upward(kind, level):
        return block_copy(kind, level, y, rise_sem, above)

    def downward(kind, level):
        return block_copy(kind, level, y, fall_sem, below)

    def begin(kind):
        @pl.when(z < depth - 1)
        def _():
            upward(kind, z).start()

        @pl.when(z > 0)
        def _():
            downward(kind, z).start()

        to_pair(kind, z).start()

    def relay(kind, step):
        @pl.when(z - step >= 0)
        def _():
            level = z - step
            upward(kind, level).wait_recv()

            @pl.when(z < depth - 1)
            def _():
                upward(kind, level).start()

            to_pair(kind, level).start()

        @pl.when(z + step <= depth - 1)
        def _():
            level = z + step
            downward(kind, level).wait_recv()

            @pl.when(z > 0)
            def _():
                downward(kind, level).start()

            to_pair(kind, level).start()

    def pair_arrived(kind, image):
        for at in range(depth // 2):
            block_copy(kind, image * (depth // 2) + at, 1 - y, pair_sem, pair).wait_recv()

    def core_copy(at):
        return pltpu.make_async_remote_copy(
            src_ref=core_send.at[at],
            dst_ref=core_recv.at[at],
            send_sem=core_out_sem.at[at],
            recv_sem=core_in_sem.at[at],
            device_id={"wid": core_peer},
            device_id_type=MESH,
        )

    def x_copy(at):
        return pltpu.make_async_remote_copy(
            src_ref=x_send.at[at],
            dst_ref=x_recv.at[at],
            send_sem=x_out_sem.at[at],
            recv_sem=x_in_sem.at[at],
            device_id={"wid": x_peer},
            device_id_type=MESH,
        )

    def combine(at):
        core_copy(at).wait_recv()
        subtotal = total[at] + core_recv[at].astype(jnp.float32)
        total[at] = subtotal
        x_send[at] = subtotal.astype(jnp.bfloat16)
        x_copy(at).start()

    def place(image, at, part):
        @pl.when(image == core)
        def _():
            total[at] = part

            @pl.when(at > 0)
            def _():
                combine(at - 1)

        @pl.when(image != core)
        def _():
            core_send[at] = part.astype(jnp.bfloat16)
            core_copy(at).start()

    def rows_of(kind, image):
        rows = gathered[kind][pl.ds(image * depth, depth)]
        return rows.reshape(rows.shape[0] * rows.shape[1], rows.shape[2])

    def turned(rows, weight):
        return lax.dot_general(
            rows, weight, (((1,), (1,)), ((), ())), preferred_element_type=jnp.float32
        )

    def straight(rows, weight):
        return jnp.dot(rows, weight, preferred_element_type=jnp.float32)

    def span(at):
        return pl.ds(pl.multiple_of(at * width, width), width)

    first_qkv = out_n + down_n
    first_up = first_qkv + 3

    def cot_products(image):
        @pl.loop(0, out_n)
        def _(at):
            place(image, at, turned(rows_of(0, image), out_w[span(at), :]))

        @pl.loop(0, down_n)
        def _(at):
            place(image, out_n + at, turned(rows_of(0, image), down_w[span(at), :]))

    def normed_products(image):
        @pl.loop(0, 3)
        def _(at):
            place(image, first_qkv + at, straight(rows_of(1, image), qkv_w[at]))

        @pl.loop(0, up_n)
        def _(at):
            place(image, first_up + at, straight(rows_of(1, image), up_w[:, span(at)]))

        @pl.when(image == core)
        def _():
            combine(first_up + up_n - 1)

    begin(0)
    begin(1)
    near = z // (depth // 2)
    far = 1 - near
    for step in range(1, depth // 2):
        relay(0, step)
        relay(1, step)
    late = list(range(depth // 2, depth))
    pair_arrived(0, near)
    for load in loads[:2]:
        load.wait()
    cot_products(near)
    for step in late[: len(late) // 2]:
        relay(0, step)
        relay(1, step)
    pair_arrived(1, near)
    for load in loads[2:]:
        load.wait()
    normed_products(near)
    for step in late[len(late) // 2 :]:
        relay(0, step)
        relay(1, step)
    pair_arrived(0, far)
    cot_products(far)
    pair_arrived(1, far)
    normed_products(far)

    @pl.loop(0, first_up + up_n)
    def _(at):
        x_copy(at).wait_recv()
        total[at] = total[at] + x_recv[at].astype(jnp.float32)

    @pl.loop(0, first_up + up_n)
    def _(at):
        core_copy(at).wait_send()
        x_copy(at).wait_send()

    for kind in range(2):
        for level in range(depth):
            to_pair(kind, level).wait_send()

            @pl.when((z < depth - 1) & (level <= z))
            def _():
                upward(kind, level).wait_send()

            @pl.when((z > 0) & (level >= z))
            def _():
                downward(kind, level).wait_send()


def forward_products(cotangent, normed, out_weight, down_weight, qkv_weight, up_weight):
    blocks = lax.axis_size("hid")
    depth = blocks // 2
    rows, columns = cotangent.shape
    width = min(CHUNK, out_weight.shape[0])
    out_n, down_n, up_n = (
        out_weight.shape[0] // width,
        down_weight.shape[0] // width,
        up_weight.shape[1] // width,
    )
    assert qkv_weight.shape[2] == width
    count = out_n + down_n + 3 + up_n
    half = rows * depth
    vmem = pl.BlockSpec(memory_space=pltpu.VMEM)
    hbm = pl.BlockSpec(memory_space=pl.ANY)
    all_shape = jax.ShapeDtypeStruct((blocks, rows, columns), jnp.bfloat16)
    weights = (out_weight, down_weight, qkv_weight, up_weight)
    slots = pltpu.VMEM((count, half, width), jnp.bfloat16)
    macs = 2 * half * columns * width * count
    return pl.pallas_call(
        functools.partial(forward_kernel, (depth, out_n, down_n, up_n, width)),
        out_shape=(
            all_shape,
            all_shape,
            jax.ShapeDtypeStruct((count, half, width), jnp.float32),
        ),
        in_specs=[vmem, vmem, hbm, hbm, hbm, hbm],
        out_specs=(vmem, vmem, vmem),
        scratch_shapes=[pltpu.VMEM(weight.shape, weight.dtype) for weight in weights]
        + [slots] * 4
        + [
            pltpu.SemaphoreType.DMA((4,)),
            pltpu.SemaphoreType.DMA((2, blocks)),
            pltpu.SemaphoreType.DMA((2, depth)),
            pltpu.SemaphoreType.DMA((2, depth)),
            pltpu.SemaphoreType.DMA((2, depth)),
            pltpu.SemaphoreType.DMA((count,)),
            pltpu.SemaphoreType.DMA((count,)),
            pltpu.SemaphoreType.DMA((count,)),
            pltpu.SemaphoreType.DMA((count,)),
        ],
        compiler_params=pltpu.CompilerParams(
            collective_id=0, has_side_effects=True, vmem_limit_bytes=56 * 1024 * 1024
        ),
        cost_estimate=pl.CostEstimate(
            flops=2 * macs, bytes_accessed=32 * 1024 * 1024, transcendentals=0
        ),
        name="forward_products",
    )(cotangent, normed, *weights)


def scatter_sum(partial):
    size = lax.axis_size("hid")
    depth = size // 2
    index = lax.axis_index("hid")
    z, y = index // 2, index % 2
    blocks = partial.reshape(depth, 2, partial.shape[0] // size, partial.shape[1])
    mine = lax.dynamic_index_in_dim(blocks, y, axis=1, keepdims=False)
    given = lax.dynamic_index_in_dim(blocks, 1 - y, axis=1, keepdims=False)
    mine = mine + swapped(given.astype(jnp.bfloat16), "hid", 1).astype(jnp.float32)

    def share(level):
        return lax.dynamic_index_in_dim(mine, level, axis=0, keepdims=False)

    result = share(z)
    for way in (1, -1):
        pairs = [
            (at, at + 2 * way) for at in range(size) if 0 <= at + 2 * way < size
        ]
        flow = None
        for far in range(depth - 1, 0, -1):
            part = share(jnp.clip(z + way * far, 0, depth - 1))
            flow = part if flow is None else flow + part
            flow = lax.ppermute(flow.astype(jnp.bfloat16), "hid", pairs).astype(jnp.float32)
        result = result + flow
    return result


def both_halves(own):
    return jnp.concatenate([own, swapped(own, "wid", 1)], axis=0)


def local(
    inputs,
    cotangent,
    norm_gain,
    qkv_weight,
    out_weight,
    up_weight,
    down_weight,
    query_gain,
    key_gain,
):
    core = lax.axis_index("wid") % 2
    input_rows = inputs.astype(jnp.float32)
    centre, inverse, total_count = row_moments(input_rows)
    inverse = inverse[:, None]
    unit_rows = (input_rows - centre[:, None]) * inverse
    normed = (unit_rows * norm_gain).astype(jnp.bfloat16)
    grad_all, normed_all, total = forward_products(
        cotangent,
        normed,
        out_weight,
        down_weight,
        jnp.transpose(qkv_weight, (1, 0, 2)),
        up_weight,
    )
    for bit in axis_bits("wid")[2:]:
        total = total + swapped(total.astype(jnp.bfloat16), "wid", bit).astype(jnp.float32)
    grad_all = grad_all.reshape(-1, grad_all.shape[2])
    normed_all = normed_all.reshape(-1, normed_all.shape[2])
    grad_order = jnp.concatenate(halves(grad_all, core), axis=0)
    normed_order = jnp.concatenate(halves(normed_all, core), axis=0)
    out_n = out_weight.shape[0] // total.shape[2]
    down_n = down_weight.shape[0] // total.shape[2]

    def side_by_side(pieces):
        return jnp.concatenate(list(pieces), axis=1)

    att_grad = side_by_side(total[:out_n]).astype(jnp.bfloat16)
    qkv_rows = jnp.transpose(total[out_n + down_n : out_n + down_n + 3], (1, 0, 2))
    hidden, pre_grad = [], []
    for at in range(down_n):
        hidden_own, pre_own = gelu_pair(total[out_n + down_n + 3 + at], total[out_n + at])
        hidden.append(hidden_own)
        pre_grad.append(pre_own)
    pre_grad = both_halves(side_by_side(pre_grad))
    attended, qkv_back = attention_pair(qkv_rows, att_grad, query_gain, key_gain)
    qkv_back = both_halves(qkv_back)
    hidden = both_halves(side_by_side(hidden))
    attended = both_halves(attended)
    normed_grad = product("tf,df->td", pre_grad, up_weight) + product(
        "tch,dch->td", qkv_back, qkv_weight
    )
    normed_grad = scatter_sum(jnp.concatenate(halves(normed_grad, core), axis=0))
    qkv_grad = product("td,tch->dch", normed_order, qkv_back).astype(jnp.bfloat16)
    out_grad = product("th,td->hd", attended, grad_order).astype(jnp.bfloat16)
    up_grad = product("td,tf->df", normed_order, pre_grad).astype(jnp.bfloat16)
    down_grad = product("tf,td->fd", hidden, grad_order).astype(jnp.bfloat16)
    unit_grad = normed_grad * norm_gain
    grad_total, grad_project = row_totals(
        jnp.stack([jnp.sum(unit_grad, axis=-1), jnp.sum(unit_grad * unit_rows, axis=-1)])
    )
    input_grad = (
        inverse
        * (
            unit_grad
            - (grad_total / total_count)[:, None]
            - unit_rows * (grad_project / total_count)[:, None]
        )
    ).astype(jnp.bfloat16)
    return (input_grad, qkv_grad, out_grad, up_grad, down_grad)


def solution(mesh):
    placed = (
        P("hid", "wid"),
        P("hid", "wid"),
        P("wid"),
        P("wid", None, "hid"),
        P("hid", "wid"),
        P("wid", "hid"),
        P("hid", "wid"),
        P(),
        P(),
    )
    return jax.shard_map(
        local,
        mesh=mesh,
        in_specs=placed,
        out_specs=(
            P("hid", "wid"),
            P("wid", None, "hid"),
            P("hid", "wid"),
            P("wid", "hid"),
            P("hid", "wid"),
        ),
        check_vma=False,
    )
```

```python
import functools
import math

import jax
import jax.numpy as jnp
from jax import lax
from jax.experimental import pallas as pl
from jax.experimental.pallas import tpu as pltpu
from jax.sharding import PartitionSpec as P

HEAD_DIM = 128
PATCHES = 256


EPSILON = 1e-06


def swapped(value, axis, bit):
    size = lax.axis_size(axis)
    return lax.ppermute(value, axis, [(at, at ^ bit) for at in range(size)])


def axis_bits(axis):
    size = lax.axis_size(axis)
    return [1 << at for at in range(size.bit_length() - 1)]


def product(form, left_arr, right_arr):
    return jnp.einsum(form, left_arr, right_arr, preferred_element_type=jnp.float32)


def head_norm(values, gain):
    centre = jnp.mean(values, axis=-1, keepdims=True)
    centred = values - centre
    inverse = lax.rsqrt(jnp.mean(centred * centred, axis=-1, keepdims=True) + EPSILON)
    unit_rows = centred * inverse
    return (unit_rows, inverse, unit_rows * gain)


def head_norm_back(upstream, unit_rows, inverse, gain):
    scaled = upstream * gain
    return inverse * (
        scaled
        - jnp.mean(scaled, axis=-1, keepdims=True)
        - unit_rows * jnp.mean(scaled * unit_rows, axis=-1, keepdims=True)
    )


def attention_pair(qkv_rows, att_grad, query_gain, key_gain):
    tok_count = qkv_rows.shape[0]
    head_width = qkv_rows.shape[2]
    head_count = head_width // HEAD_DIM
    image_count = tok_count // PATCHES
    score_scale = 1.0 / math.sqrt(HEAD_DIM)

    def per_image(values):
        return values.reshape(image_count, PATCHES, head_count, HEAD_DIM)

    query_unit, query_inverse, query_normed = head_norm(per_image(qkv_rows[:, 0]), query_gain)
    key_unit, key_inverse, key_normed = head_norm(per_image(qkv_rows[:, 1]), key_gain)
    query_normed = query_normed.astype(jnp.bfloat16)
    key_normed = key_normed.astype(jnp.bfloat16)
    value_rows = per_image(qkv_rows[:, 2]).astype(jnp.bfloat16)
    scores = product("ipha,iqha->ihpq", query_normed, key_normed) * score_scale
    exponent = jnp.exp(scores)
    probs = exponent / jnp.sum(exponent, axis=-1, keepdims=True)
    probs_low = probs.astype(jnp.bfloat16)
    attended = (
        product("ihpq,iqha->ipha", probs_low, value_rows)
        .astype(jnp.bfloat16)
        .reshape(tok_count, head_width)
    )
    grad_rows = per_image(att_grad)
    probs_grad = product("ipha,iqha->ihpq", grad_rows, value_rows)
    value_grad = product("ihpq,ipha->iqha", probs_low, grad_rows)
    score_grad = (
        probs * (probs_grad - jnp.sum(probs * probs_grad, axis=-1, keepdims=True)) * score_scale
    ).astype(jnp.bfloat16)
    qn_grad = product("ihpq,iqha->ipha", score_grad, key_normed)
    kn_grad = product("ihpq,ipha->iqha", score_grad, query_normed)
    query_grad = head_norm_back(qn_grad, query_unit, query_inverse, query_gain)
    key_grad = head_norm_back(kn_grad, key_unit, key_inverse, key_gain)
    qkv_back = jnp.stack(
        [
            query_grad.reshape(tok_count, head_width),
            key_grad.reshape(tok_count, head_width),
            value_grad.reshape(tok_count, head_width),
        ],
        axis=1,
    ).astype(jnp.bfloat16)
    return (attended, qkv_back)


def row_moments(input_rows):
    count = float(input_rows.shape[1])
    mean = jnp.mean(input_rows, axis=-1)
    deviation = input_rows - mean[:, None]
    square = jnp.sum(deviation * deviation, axis=-1)
    for bit in axis_bits("wid"):
        other_mean, other_square = swapped(jnp.stack([mean, square]), "wid", bit)
        offset = other_mean - mean
        mean = 0.5 * (mean + other_mean)
        square = square + other_square + offset * offset * (0.5 * count)
        count = 2.0 * count
    return (mean, lax.rsqrt(square / count + EPSILON), count)


def row_totals(sums):
    for bit in axis_bits("wid"):
        sums = sums + swapped(sums, "wid", bit)
    return sums


MESH = pl.DeviceIdType.MESH
GELU_SLOPE = math.sqrt(2.0 / math.pi)
GELU_CUBE = 0.044715


def gelu_both(pre_act, upstream):
    square = pre_act * pre_act
    bend = jnp.tanh(GELU_SLOPE * pre_act * (1.0 + GELU_CUBE * square))
    lift = 0.5 * (1.0 + bend)
    slope = GELU_SLOPE * (1.0 + 3.0 * GELU_CUBE * square)
    derivative = lift + 0.5 * pre_act * (1.0 - bend * bend) * slope
    return (pre_act * lift, derivative * upstream)


CHUNK = 512


def forward_kernel(
    sizes,
    cot_ref,
    normed_ref,
    out_ref,
    down_ref,
    qkv_ref,
    up_ref,
    cot_all,
    normed_all,
    att_out,
    qkv_out,
    hidden_all,
    pre_all,
    total,
    out_w,
    down_w,
    qkv_w,
    up_w,
    core_send,
    core_recv,
    x_send,
    x_recv,
    load_sem,
    slot_sem,
    rise_sem,
    fall_sem,
    pair_sem,
    core_out_sem,
    core_in_sem,
    x_out_sem,
    x_in_sem,
    hand_out_sem,
    hand_in_sem,
):
    depth, out_n, down_n, up_n, width, stages = sizes
    hid, wid = lax.axis_index("hid"), lax.axis_index("wid")
    z, y = hid // 2, hid % 2
    core = wid % 2
    above, below, pair = hid + 2, hid - 2, z * 2 + 1 - y
    core_peer = wid + 1 - 2 * core
    x_peers = [
        wid + bit - 2 * bit * ((wid // bit) % 2) for bit in (2 << at for at in range(stages))
    ]

    loads = [
        pltpu.make_async_copy(src, dst, load_sem.at[at])
        for at, (src, dst) in enumerate(
            [(out_ref, out_w), (down_ref, down_w), (qkv_ref, qkv_w), (up_ref, up_w)]
        )
    ]
    for load in loads:
        load.start()

    gathered = (cot_all, normed_all)
    cot_all[hid] = cot_ref[...]
    normed_all[hid] = normed_ref[...]

    barrier = pltpu.get_barrier_semaphore()
    pl.semaphore_signal(barrier, inc=1, device_id={"hid": pair}, device_id_type=MESH)
    pl.semaphore_signal(barrier, inc=1, device_id={"wid": core_peer}, device_id_type=MESH)
    for peer in x_peers:
        pl.semaphore_signal(barrier, inc=1, device_id={"wid": peer}, device_id_type=MESH)

    @pl.when(z < depth - 1)
    def _():
        pl.semaphore_signal(barrier, inc=1, device_id={"hid": above}, device_id_type=MESH)

    @pl.when(z > 0)
    def _():
        pl.semaphore_signal(barrier, inc=1, device_id={"hid": below}, device_id_type=MESH)

    neighbours = 2 + stages + jnp.where(z > 0, 1, 0) + jnp.where(z < depth - 1, 1, 0)
    pl.semaphore_wait(barrier, neighbours)

    def block_copy(kind, level, side, sems, target):
        slot = level * 2 + side
        return pltpu.make_async_remote_copy(
            src_ref=gathered[kind].at[slot],
            dst_ref=gathered[kind].at[slot],
            send_sem=sems.at[kind, level],
            recv_sem=slot_sem.at[kind, slot],
            device_id={"hid": target},
            device_id_type=MESH,
        )

    def to_pair(kind, level):
        return block_copy(kind, level, y, pair_sem, pair)

    def upward(kind, level):
        return block_copy(kind, level, y, rise_sem, above)

    def downward(kind, level):
        return block_copy(kind, level, y, fall_sem, below)

    def begin(kind):
        @pl.when(z < depth - 1)
        def _():
            upward(kind, z).start()

        @pl.when(z > 0)
        def _():
            downward(kind, z).start()

        to_pair(kind, z).start()

    def relay(kind, step):
        @pl.when(z - step >= 0)
        def _():
            level = z - step
            upward(kind, level).wait_recv()

            @pl.when(z < depth - 1)
            def _():
                upward(kind, level).start()

            to_pair(kind, level).start()

        @pl.when(z + step <= depth - 1)
        def _():
            level = z + step
            downward(kind, level).wait_recv()

            @pl.when(z > 0)
            def _():
                downward(kind, level).start()

            to_pair(kind, level).start()

    def pair_arrived(kind, image):
        for at in range(depth // 2):
            block_copy(kind, image * (depth // 2) + at, 1 - y, pair_sem, pair).wait_recv()

    def core_copy(at):
        return pltpu.make_async_remote_copy(
            src_ref=core_send.at[at],
            dst_ref=core_recv.at[at],
            send_sem=core_out_sem.at[at],
            recv_sem=core_in_sem.at[at],
            device_id={"wid": core_peer},
            device_id_type=MESH,
        )

    def x_copy(at, stage=0):
        return pltpu.make_async_remote_copy(
            src_ref=x_send.at[stage, at],
            dst_ref=x_recv.at[stage, at],
            send_sem=x_out_sem.at[stage, at],
            recv_sem=x_in_sem.at[stage, at],
            device_id={"wid": x_peers[stage]},
            device_id_type=MESH,
        )

    def combine(at):
        core_copy(at).wait_recv()
        subtotal = total[at] + core_recv[at].astype(jnp.float32)
        total[at] = subtotal
        x_send[0, at] = subtotal.astype(jnp.bfloat16)
        x_copy(at).start()

    def place(image, at, part):
        @pl.when(image == core)
        def _():
            total[at] = part

            @pl.when(at > 0)
            def _():
                combine(at - 1)

        @pl.when(image != core)
        def _():
            core_send[at] = part.astype(jnp.bfloat16)
            core_copy(at).start()

    def rows_of(kind, image):
        rows = gathered[kind][pl.ds(image * depth, depth)]
        return rows.reshape(rows.shape[0] * rows.shape[1], rows.shape[2])

    def turned(rows, weight):
        return lax.dot_general(
            rows, weight, (((1,), (1,)), ((), ())), preferred_element_type=jnp.float32
        )

    def straight(rows, weight):
        return jnp.dot(rows, weight, preferred_element_type=jnp.float32)

    def span(at):
        return pl.ds(pl.multiple_of(at * width, width), width)

    first_qkv = out_n + down_n
    first_up = first_qkv + 3

    def cot_products(image):
        @pl.loop(0, out_n)
        def _(at):
            place(image, at, turned(rows_of(0, image), out_w[span(at), :]))

        @pl.loop(0, down_n)
        def _(at):
            place(image, out_n + at, turned(rows_of(0, image), down_w[span(at), :]))

    def qkv_products(image):
        @pl.loop(0, 3)
        def _(at):
            place(image, first_qkv + at, straight(rows_of(1, image), qkv_w[at]))

    def up_products(image):
        @pl.loop(0, up_n)
        def _(at):
            place(image, first_up + at, straight(rows_of(1, image), up_w[:, span(at)]))

        @pl.when(image == core)
        def _():
            combine(first_up + up_n - 1)

    def hand_copy(kind, at, image):
        block = ((hidden_all, pre_all)[kind]).at[image_rows(image), span(at)]
        return pltpu.make_async_remote_copy(
            src_ref=block,
            dst_ref=block,
            send_sem=hand_out_sem.at[kind, at],
            recv_sem=hand_in_sem.at[kind, at],
            device_id={"wid": core_peer},
            device_id_type=MESH,
        )

    def image_rows(image):
        half = total.shape[1]
        return pl.ds(pl.multiple_of(image * half, half), half)

    begin(0)
    begin(1)
    near = z // (depth // 2)
    far = 1 - near
    for step in range(1, depth // 2):
        relay(0, step)
        relay(1, step)
    late = list(range(depth // 2, depth))
    pair_arrived(0, near)
    for load in loads[:2]:
        load.wait()
    cot_products(near)
    for step in late[: len(late) // 2]:
        relay(0, step)
        relay(1, step)
    pair_arrived(1, near)
    for load in loads[2:]:
        load.wait()
    qkv_products(near)
    for step in late[len(late) // 2 :]:
        relay(0, step)
        relay(1, step)
    up_products(near)
    pair_arrived(0, far)
    cot_products(far)
    pair_arrived(1, far)
    qkv_products(far)
    up_products(far)

    def arrived(at, stage):
        x_copy(at, stage).wait_recv()
        return total[at] + x_recv[stage, at].astype(jnp.float32)

    for stage in range(stages - 1):

        @pl.loop(0, first_up + up_n)
        def _(at):
            subtotal = arrived(at, stage)
            total[at] = subtotal
            x_send[stage + 1, at] = subtotal.astype(jnp.bfloat16)
            x_copy(at, stage + 1).start()

    last = stages - 1
    for at in range(out_n):
        att_out[:, at * width : (at + 1) * width] = arrived(at, last).astype(jnp.bfloat16)

    @pl.loop(0, down_n)
    def _(at):
        total[out_n + at] = arrived(out_n + at, last)

    @pl.loop(0, 3)
    def _(at):
        qkv_out[at] = arrived(first_qkv + at, last)

    @pl.loop(0, up_n)
    def _(at):
        hidden, pre_grad = gelu_both(arrived(first_up + at, last), total[out_n + at])
        hidden_all[image_rows(core), span(at)] = hidden.astype(jnp.bfloat16)
        pre_all[image_rows(core), span(at)] = pre_grad.astype(jnp.bfloat16)
        hand_copy(1, at, core).start()
        hand_copy(0, at, core).start()

    @pl.loop(0, up_n)
    def _(at):
        hand_copy(1, at, 1 - core).wait_recv()
        hand_copy(0, at, 1 - core).wait_recv()
        hand_copy(1, at, core).wait_send()
        hand_copy(0, at, core).wait_send()

    @pl.loop(0, first_up + up_n)
    def _(at):
        core_copy(at).wait_send()
        for stage in range(stages):
            x_copy(at, stage).wait_send()

    for kind in range(2):
        for level in range(depth):
            to_pair(kind, level).wait_send()

            @pl.when((z < depth - 1) & (level <= z))
            def _():
                upward(kind, level).wait_send()

            @pl.when((z > 0) & (level >= z))
            def _():
                downward(kind, level).wait_send()


def forward_products(cotangent, normed, out_weight, down_weight, qkv_weight, up_weight):
    blocks = lax.axis_size("hid")
    depth = blocks // 2
    rows, columns = cotangent.shape
    width = min(CHUNK, out_weight.shape[0])
    out_n, down_n, up_n = (
        out_weight.shape[0] // width,
        down_weight.shape[0] // width,
        up_weight.shape[1] // width,
    )
    assert qkv_weight.shape[2] == width
    count = out_n + down_n + 3 + up_n
    half = rows * depth
    stages = lax.axis_size("wid").bit_length() - 2
    vmem = pl.BlockSpec(memory_space=pltpu.VMEM)
    hbm = pl.BlockSpec(memory_space=pl.ANY)
    all_shape = jax.ShapeDtypeStruct((blocks, rows, columns), jnp.bfloat16)
    weights = (out_weight, down_weight, qkv_weight, up_weight)
    slots = pltpu.VMEM((count, half, width), jnp.bfloat16)
    macs = 2 * half * columns * width * count
    return pl.pallas_call(
        functools.partial(forward_kernel, (depth, out_n, down_n, up_n, width, stages)),
        out_shape=(
            all_shape,
            all_shape,
            jax.ShapeDtypeStruct((half, out_weight.shape[0]), jnp.bfloat16),
            jax.ShapeDtypeStruct((3, half, width), jnp.float32),
            jax.ShapeDtypeStruct((2 * half, up_weight.shape[1]), jnp.bfloat16),
            jax.ShapeDtypeStruct((2 * half, up_weight.shape[1]), jnp.bfloat16),
        ),
        in_specs=[vmem, vmem, hbm, hbm, hbm, hbm],
        out_specs=(vmem,) * 6,
        scratch_shapes=[pltpu.VMEM((count, half, width), jnp.float32)]
        + [pltpu.VMEM(weight.shape, weight.dtype) for weight in weights]
        + [slots] * 2
        + [pltpu.VMEM((stages, count, half, width), jnp.bfloat16)] * 2
        + [
            pltpu.SemaphoreType.DMA((4,)),
            pltpu.SemaphoreType.DMA((2, blocks)),
            pltpu.SemaphoreType.DMA((2, depth)),
            pltpu.SemaphoreType.DMA((2, depth)),
            pltpu.SemaphoreType.DMA((2, depth)),
            pltpu.SemaphoreType.DMA((count,)),
            pltpu.SemaphoreType.DMA((count,)),
            pltpu.SemaphoreType.DMA((stages, count)),
            pltpu.SemaphoreType.DMA((stages, count)),
            pltpu.SemaphoreType.DMA((2, up_n)),
            pltpu.SemaphoreType.DMA((2, up_n)),
        ],
        compiler_params=pltpu.CompilerParams(
            collective_id=0, has_side_effects=True, vmem_limit_bytes=56 * 1024 * 1024
        ),
        cost_estimate=pl.CostEstimate(
            flops=2 * macs, bytes_accessed=32 * 1024 * 1024, transcendentals=0
        ),
        name="forward_products",
    )(cotangent, normed, *weights)


def scatter_sums(first, second, works):
    size = lax.axis_size("hid")
    depth = size // 2
    index = lax.axis_index("hid")
    z, y = index // 2, index % 2
    ways = (1, -1)

    def split(partial):
        return partial.reshape(depth, 2, partial.shape[0] // size, partial.shape[1])

    def along(value, at, axis):
        return lax.dynamic_index_in_dim(value, at, axis=axis, keepdims=False)

    def shifted(flow, way):
        pairs = [(at, at + 2 * way) for at in range(size) if 0 <= at + 2 * way < size]
        return lax.ppermute(flow.astype(jnp.bfloat16), "hid", pairs)

    def swap_of(blocks, axis):
        return swapped(along(blocks, 1 - y, axis).astype(jnp.bfloat16), "hid", 1)

    def chain_step(blocks, flows, far):
        parts = [along(blocks, jnp.clip(z + way * far, 0, depth - 1), 0) for way in ways]
        if flows is not None:
            parts = [part + flow.astype(jnp.float32) for part, flow in zip(parts, flows)]
        return [shifted(part, way) for part, way in zip(parts, ways)]

    def chain_end(blocks, flows):
        up, down = (flow.astype(jnp.float32) for flow in flows)
        return along(blocks, z, 0) + up + down

    first, second = split(first), split(second)
    done = []
    first_flows, second_flows = None, None
    for turn in range(depth):
        if turn == 0:
            first_got = [swap_of(first, 1)]
        else:
            first_flows = first_got = chain_step(first, first_flows, depth - turn)
        if turn < depth - 1:
            second_flows = second_got = chain_step(second, second_flows, depth - 1 - turn)
        else:
            second = chain_end(second, second_flows)
            second_got = [swap_of(second, 0)]
        if turn < len(works):
            first_got, second_got, work = lax.optimization_barrier(
                (first_got, second_got, works[turn]())
            )
            done.append(work)
        if turn == 0:
            first = along(first, y, 1) + first_got[0].astype(jnp.float32)
        else:
            first_flows = first_got
        if turn < depth - 1:
            second_flows = second_got
        else:
            second = along(second, y, 0) + second_got[0].astype(jnp.float32)
    first = chain_end(first, first_flows)
    return (jnp.concatenate([first, second], axis=1), done)


def both_halves(own, core):
    other = swapped(own, "wid", 1)
    return jnp.concatenate(
        [jnp.where(core == 0, own, other), jnp.where(core == 0, other, own)], axis=0
    )


def local(
    inputs,
    cotangent,
    norm_gain,
    qkv_weight,
    out_weight,
    up_weight,
    down_weight,
    query_gain,
    key_gain,
):
    core = lax.axis_index("wid") % 2
    input_rows = inputs.astype(jnp.float32)
    centre, inverse, total_count = row_moments(input_rows)
    inverse = inverse[:, None]
    unit_rows = (input_rows - centre[:, None]) * inverse
    normed = (unit_rows * norm_gain).astype(jnp.bfloat16)
    grad_all, normed_all, att_grad, qkv_rows, hidden, pre_grad = forward_products(
        cotangent,
        normed,
        out_weight,
        down_weight,
        jnp.transpose(qkv_weight, (1, 0, 2)),
        up_weight,
    )
    grad_all = grad_all.reshape(-1, grad_all.shape[2])
    normed_all = normed_all.reshape(-1, normed_all.shape[2])
    attended, qkv_back = attention_pair(
        jnp.transpose(qkv_rows, (1, 0, 2)), att_grad, query_gain, key_gain
    )
    qkv_back = both_halves(qkv_back, core)
    attended = both_halves(attended, core)

    def normed_part(span):
        return product("tf,df->td", pre_grad, up_weight[span]) + product(
            "tch,dch->td", qkv_back, qkv_weight[span]
        )

    middle = up_weight.shape[0] // 2
    normed_grad, (up_grad, down_grad, qkv_grad, out_grad) = scatter_sums(
        normed_part(slice(None, middle)),
        normed_part(slice(middle, None)),
        (
            lambda: product("td,tf->df", normed_all, pre_grad).astype(jnp.bfloat16),
            lambda: product("tf,td->fd", hidden, grad_all).astype(jnp.bfloat16),
            lambda: product("td,tch->dch", normed_all, qkv_back).astype(jnp.bfloat16),
            lambda: product("th,td->hd", attended, grad_all).astype(jnp.bfloat16),
        ),
    )
    unit_grad = normed_grad * norm_gain
    grad_total, grad_project = row_totals(
        jnp.stack([jnp.sum(unit_grad, axis=-1), jnp.sum(unit_grad * unit_rows, axis=-1)])
    )
    input_grad = (
        inverse
        * (
            unit_grad
            - (grad_total / total_count)[:, None]
            - unit_rows * (grad_project / total_count)[:, None]
        )
    ).astype(jnp.bfloat16)
    return (input_grad, qkv_grad, out_grad, up_grad, down_grad)


def solution(mesh):
    placed = (
        P("hid", "wid"),
        P("hid", "wid"),
        P("wid"),
        P("wid", None, "hid"),
        P("hid", "wid"),
        P("wid", "hid"),
        P("hid", "wid"),
        P(),
        P(),
    )
    return jax.shard_map(
        local,
        mesh=mesh,
        in_specs=placed,
        out_specs=(
            P("hid", "wid"),
            P("wid", None, "hid"),
            P("hid", "wid"),
            P("wid", "hid"),
            P("hid", "wid"),
        ),
        check_vma=False,
    )
```

```python
import functools
import math

import jax
import jax.numpy as jnp
from jax import lax
from jax.experimental import pallas as pl
from jax.experimental.pallas import tpu as pltpu
from jax.sharding import PartitionSpec as P

HEAD_DIM = 128
PATCHES = 256


EPSILON = 1e-06


def swapped(value, axis, bit):
    size = lax.axis_size(axis)
    return lax.ppermute(value, axis, [(at, at ^ bit) for at in range(size)])


def axis_bits(axis):
    size = lax.axis_size(axis)
    return [1 << at for at in range(size.bit_length() - 1)]


def product(form, left_arr, right_arr):
    return jnp.einsum(form, left_arr, right_arr, preferred_element_type=jnp.float32)


def head_norm(values, gain):
    centre = jnp.mean(values, axis=-1, keepdims=True)
    centred = values - centre
    inverse = lax.rsqrt(jnp.mean(centred * centred, axis=-1, keepdims=True) + EPSILON)
    unit_rows = centred * inverse
    return (unit_rows, inverse, unit_rows * gain)


def head_norm_back(upstream, unit_rows, inverse, gain):
    scaled = upstream * gain
    return inverse * (
        scaled
        - jnp.mean(scaled, axis=-1, keepdims=True)
        - unit_rows * jnp.mean(scaled * unit_rows, axis=-1, keepdims=True)
    )


def attention_pair(qkv_rows, att_grad, query_gain, key_gain):
    tok_count = qkv_rows.shape[0]
    head_width = qkv_rows.shape[2]
    head_count = head_width // HEAD_DIM
    image_count = tok_count // PATCHES
    score_scale = 1.0 / math.sqrt(HEAD_DIM)

    def per_image(values):
        return values.reshape(image_count, PATCHES, head_count, HEAD_DIM)

    query_unit, query_inverse, query_normed = head_norm(per_image(qkv_rows[:, 0]), query_gain)
    key_unit, key_inverse, key_normed = head_norm(per_image(qkv_rows[:, 1]), key_gain)
    query_normed = query_normed.astype(jnp.bfloat16)
    key_normed = key_normed.astype(jnp.bfloat16)
    value_rows = per_image(qkv_rows[:, 2]).astype(jnp.bfloat16)
    scores = product("ipha,iqha->ihpq", query_normed, key_normed) * score_scale
    exponent = jnp.exp(scores)
    probs = exponent / jnp.sum(exponent, axis=-1, keepdims=True)
    probs_low = probs.astype(jnp.bfloat16)
    attended = (
        product("ihpq,iqha->ipha", probs_low, value_rows)
        .astype(jnp.bfloat16)
        .reshape(tok_count, head_width)
    )
    grad_rows = per_image(att_grad)
    probs_grad = product("ipha,iqha->ihpq", grad_rows, value_rows)
    value_grad = product("ihpq,ipha->iqha", probs_low, grad_rows)
    score_grad = (
        probs * (probs_grad - jnp.sum(probs * probs_grad, axis=-1, keepdims=True)) * score_scale
    ).astype(jnp.bfloat16)
    qn_grad = product("ihpq,iqha->ipha", score_grad, key_normed)
    kn_grad = product("ihpq,ipha->iqha", score_grad, query_normed)
    query_grad = head_norm_back(qn_grad, query_unit, query_inverse, query_gain)
    key_grad = head_norm_back(kn_grad, key_unit, key_inverse, key_gain)
    qkv_back = jnp.stack(
        [
            query_grad.reshape(tok_count, head_width),
            key_grad.reshape(tok_count, head_width),
            value_grad.reshape(tok_count, head_width),
        ],
        axis=1,
    ).astype(jnp.bfloat16)
    return (attended, qkv_back)


def row_moments(input_rows):
    count = float(input_rows.shape[1])
    mean = jnp.mean(input_rows, axis=-1)
    deviation = input_rows - mean[:, None]
    square = jnp.sum(deviation * deviation, axis=-1)
    for bit in axis_bits("wid"):
        other_mean, other_square = swapped(jnp.stack([mean, square]), "wid", bit)
        offset = other_mean - mean
        mean = 0.5 * (mean + other_mean)
        square = square + other_square + offset * offset * (0.5 * count)
        count = 2.0 * count
    return (mean, lax.rsqrt(square / count + EPSILON))


MESH = pl.DeviceIdType.MESH
GELU_SLOPE = math.sqrt(2.0 / math.pi)
GELU_CUBE = 0.044715


def gelu_both(pre_act, upstream):
    square = pre_act * pre_act
    bend = jnp.tanh(GELU_SLOPE * pre_act * (1.0 + GELU_CUBE * square))
    lift = 0.5 * (1.0 + bend)
    slope = GELU_SLOPE * (1.0 + 3.0 * GELU_CUBE * square)
    derivative = lift + 0.5 * pre_act * (1.0 - bend * bend) * slope
    return (pre_act * lift, derivative * upstream)


CHUNK = 512


def forward_kernel(
    sizes,
    cot_ref,
    normed_ref,
    out_ref,
    down_ref,
    qkv_ref,
    up_ref,
    cot_all,
    normed_all,
    att_out,
    qkv_out,
    hidden_all,
    pre_all,
    total,
    out_w,
    down_w,
    qkv_w,
    up_w,
    core_send,
    core_recv,
    x_send,
    x_recv,
    load_sem,
    slot_sem,
    rise_sem,
    fall_sem,
    pair_sem,
    core_out_sem,
    core_in_sem,
    x_out_sem,
    x_in_sem,
    hand_out_sem,
    hand_in_sem,
):
    depth, out_n, down_n, up_n, width, stages = sizes
    hid, wid = lax.axis_index("hid"), lax.axis_index("wid")
    z, y = hid // 2, hid % 2
    core = wid % 2
    above, below, pair = hid + 2, hid - 2, z * 2 + 1 - y
    core_peer = wid + 1 - 2 * core
    x_peers = [
        wid + bit - 2 * bit * ((wid // bit) % 2) for bit in (2 << at for at in range(stages))
    ]

    loads = [
        pltpu.make_async_copy(src, dst, load_sem.at[at])
        for at, (src, dst) in enumerate(
            [(out_ref, out_w), (down_ref, down_w), (qkv_ref, qkv_w), (up_ref, up_w)]
        )
    ]
    for load in loads:
        load.start()

    gathered = (cot_all, normed_all)
    cot_all[hid] = cot_ref[...]
    normed_all[hid] = normed_ref[...]

    barrier = pltpu.get_barrier_semaphore()
    pl.semaphore_signal(barrier, inc=1, device_id={"hid": pair}, device_id_type=MESH)
    pl.semaphore_signal(barrier, inc=1, device_id={"wid": core_peer}, device_id_type=MESH)
    for peer in x_peers:
        pl.semaphore_signal(barrier, inc=1, device_id={"wid": peer}, device_id_type=MESH)

    @pl.when(z < depth - 1)
    def _():
        pl.semaphore_signal(barrier, inc=1, device_id={"hid": above}, device_id_type=MESH)

    @pl.when(z > 0)
    def _():
        pl.semaphore_signal(barrier, inc=1, device_id={"hid": below}, device_id_type=MESH)

    neighbours = 2 + stages + jnp.where(z > 0, 1, 0) + jnp.where(z < depth - 1, 1, 0)
    pl.semaphore_wait(barrier, neighbours)

    def block_copy(kind, level, side, sems, target):
        slot = level * 2 + side
        return pltpu.make_async_remote_copy(
            src_ref=gathered[kind].at[slot],
            dst_ref=gathered[kind].at[slot],
            send_sem=sems.at[kind, level],
            recv_sem=slot_sem.at[kind, slot],
            device_id={"hid": target},
            device_id_type=MESH,
        )

    def to_pair(kind, level):
        return block_copy(kind, level, y, pair_sem, pair)

    def upward(kind, level):
        return block_copy(kind, level, y, rise_sem, above)

    def downward(kind, level):
        return block_copy(kind, level, y, fall_sem, below)

    def begin(kind):
        @pl.when(z < depth - 1)
        def _():
            upward(kind, z).start()

        @pl.when(z > 0)
        def _():
            downward(kind, z).start()

        to_pair(kind, z).start()

    def relay(kind, step):
        @pl.when(z - step >= 0)
        def _():
            level = z - step
            upward(kind, level).wait_recv()

            @pl.when(z < depth - 1)
            def _():
                upward(kind, level).start()

            to_pair(kind, level).start()

        @pl.when(z + step <= depth - 1)
        def _():
            level = z + step
            downward(kind, level).wait_recv()

            @pl.when(z > 0)
            def _():
                downward(kind, level).start()

            to_pair(kind, level).start()

    def pair_arrived(kind, image):
        for at in range(depth // 2):
            block_copy(kind, image * (depth // 2) + at, 1 - y, pair_sem, pair).wait_recv()

    def core_copy(at):
        return pltpu.make_async_remote_copy(
            src_ref=core_send.at[at],
            dst_ref=core_recv.at[at],
            send_sem=core_out_sem.at[at],
            recv_sem=core_in_sem.at[at],
            device_id={"wid": core_peer},
            device_id_type=MESH,
        )

    def x_copy(at, stage=0):
        return pltpu.make_async_remote_copy(
            src_ref=x_send.at[stage, at],
            dst_ref=x_recv.at[stage, at],
            send_sem=x_out_sem.at[stage, at],
            recv_sem=x_in_sem.at[stage, at],
            device_id={"wid": x_peers[stage]},
            device_id_type=MESH,
        )

    def combine(at):
        core_copy(at).wait_recv()
        subtotal = total[at] + core_recv[at].astype(jnp.float32)
        total[at] = subtotal
        x_send[0, at] = subtotal.astype(jnp.bfloat16)
        x_copy(at).start()

    def place(image, at, part):
        @pl.when(image == core)
        def _():
            total[at] = part

            @pl.when(at > 0)
            def _():
                combine(at - 1)

        @pl.when(image != core)
        def _():
            core_send[at] = part.astype(jnp.bfloat16)
            core_copy(at).start()

    def rows_of(kind, image):
        rows = gathered[kind][pl.ds(image * depth, depth)]
        return rows.reshape(rows.shape[0] * rows.shape[1], rows.shape[2])

    def turned(rows, weight):
        return lax.dot_general(
            rows, weight, (((1,), (1,)), ((), ())), preferred_element_type=jnp.float32
        )

    def straight(rows, weight):
        return jnp.dot(rows, weight, preferred_element_type=jnp.float32)

    def span(at):
        return pl.ds(pl.multiple_of(at * width, width), width)

    first_qkv = out_n + down_n
    first_up = first_qkv + 3

    def cot_products(image):
        @pl.loop(0, out_n)
        def _(at):
            place(image, at, turned(rows_of(0, image), out_w[span(at), :]))

        @pl.loop(0, down_n)
        def _(at):
            place(image, out_n + at, turned(rows_of(0, image), down_w[span(at), :]))

    def qkv_products(image):
        @pl.loop(0, 3)
        def _(at):
            place(image, first_qkv + at, straight(rows_of(1, image), qkv_w[at]))

    def up_products(image):
        @pl.loop(0, up_n)
        def _(at):
            place(image, first_up + at, straight(rows_of(1, image), up_w[:, span(at)]))

        @pl.when(image == core)
        def _():
            combine(first_up + up_n - 1)

    def hand_copy(kind, at, image):
        block = ((hidden_all, pre_all)[kind]).at[image_rows(image), span(at)]
        return pltpu.make_async_remote_copy(
            src_ref=block,
            dst_ref=block,
            send_sem=hand_out_sem.at[kind, at],
            recv_sem=hand_in_sem.at[kind, at],
            device_id={"wid": core_peer},
            device_id_type=MESH,
        )

    def image_rows(image):
        half = total.shape[1]
        return pl.ds(pl.multiple_of(image * half, half), half)

    begin(0)
    begin(1)
    near = z // (depth // 2)
    far = 1 - near
    for step in range(1, depth // 2):
        relay(0, step)
        relay(1, step)
    late = list(range(depth // 2, depth))
    pair_arrived(0, near)
    for load in loads[:2]:
        load.wait()
    cot_products(near)
    for step in late[: len(late) // 2]:
        relay(0, step)
        relay(1, step)
    pair_arrived(1, near)
    for load in loads[2:]:
        load.wait()
    qkv_products(near)
    for step in late[len(late) // 2 :]:
        relay(0, step)
        relay(1, step)
    up_products(near)
    pair_arrived(0, far)
    cot_products(far)
    pair_arrived(1, far)
    qkv_products(far)
    up_products(far)

    def arrived(at, stage):
        x_copy(at, stage).wait_recv()
        return total[at] + x_recv[stage, at].astype(jnp.float32)

    for stage in range(stages - 1):

        @pl.loop(0, first_up + up_n)
        def _(at):
            subtotal = arrived(at, stage)
            total[at] = subtotal
            x_send[stage + 1, at] = subtotal.astype(jnp.bfloat16)
            x_copy(at, stage + 1).start()

    last = stages - 1
    for at in range(out_n):
        att_out[:, at * width : (at + 1) * width] = arrived(at, last).astype(jnp.bfloat16)

    @pl.loop(0, down_n)
    def _(at):
        total[out_n + at] = arrived(out_n + at, last)

    @pl.loop(0, 3)
    def _(at):
        qkv_out[at] = arrived(first_qkv + at, last)

    @pl.loop(0, up_n)
    def _(at):
        hidden, pre_grad = gelu_both(arrived(first_up + at, last), total[out_n + at])
        hidden_all[image_rows(core), span(at)] = hidden.astype(jnp.bfloat16)
        pre_all[image_rows(core), span(at)] = pre_grad.astype(jnp.bfloat16)
        hand_copy(1, at, core).start()
        hand_copy(0, at, core).start()

    @pl.loop(0, up_n)
    def _(at):
        hand_copy(1, at, 1 - core).wait_recv()
        hand_copy(0, at, 1 - core).wait_recv()
        hand_copy(1, at, core).wait_send()
        hand_copy(0, at, core).wait_send()

    @pl.loop(0, first_up + up_n)
    def _(at):
        core_copy(at).wait_send()
        for stage in range(stages):
            x_copy(at, stage).wait_send()

    for kind in range(2):
        for level in range(depth):
            to_pair(kind, level).wait_send()

            @pl.when((z < depth - 1) & (level <= z))
            def _():
                upward(kind, level).wait_send()

            @pl.when((z > 0) & (level >= z))
            def _():
                downward(kind, level).wait_send()


def forward_products(cotangent, normed, out_weight, down_weight, qkv_weight, up_weight):
    blocks = lax.axis_size("hid")
    depth = blocks // 2
    rows, columns = cotangent.shape
    width = min(CHUNK, out_weight.shape[0])
    out_n, down_n, up_n = (
        out_weight.shape[0] // width,
        down_weight.shape[0] // width,
        up_weight.shape[1] // width,
    )
    assert qkv_weight.shape[2] == width
    count = out_n + down_n + 3 + up_n
    half = rows * depth
    stages = lax.axis_size("wid").bit_length() - 2
    vmem = pl.BlockSpec(memory_space=pltpu.VMEM)
    hbm = pl.BlockSpec(memory_space=pl.ANY)
    all_shape = jax.ShapeDtypeStruct((blocks, rows, columns), jnp.bfloat16)
    weights = (out_weight, down_weight, qkv_weight, up_weight)
    slots = pltpu.VMEM((count, half, width), jnp.bfloat16)
    macs = 2 * half * columns * width * count
    return pl.pallas_call(
        functools.partial(forward_kernel, (depth, out_n, down_n, up_n, width, stages)),
        out_shape=(
            all_shape,
            all_shape,
            jax.ShapeDtypeStruct((half, out_weight.shape[0]), jnp.bfloat16),
            jax.ShapeDtypeStruct((3, half, width), jnp.float32),
            jax.ShapeDtypeStruct((2 * half, up_weight.shape[1]), jnp.bfloat16),
            jax.ShapeDtypeStruct((2 * half, up_weight.shape[1]), jnp.bfloat16),
        ),
        in_specs=[vmem, vmem, hbm, hbm, hbm, hbm],
        out_specs=(vmem,) * 6,
        scratch_shapes=[pltpu.VMEM((count, half, width), jnp.float32)]
        + [pltpu.VMEM(weight.shape, weight.dtype) for weight in weights]
        + [slots] * 2
        + [pltpu.VMEM((stages, count, half, width), jnp.bfloat16)] * 2
        + [
            pltpu.SemaphoreType.DMA((4,)),
            pltpu.SemaphoreType.DMA((2, blocks)),
            pltpu.SemaphoreType.DMA((2, depth)),
            pltpu.SemaphoreType.DMA((2, depth)),
            pltpu.SemaphoreType.DMA((2, depth)),
            pltpu.SemaphoreType.DMA((count,)),
            pltpu.SemaphoreType.DMA((count,)),
            pltpu.SemaphoreType.DMA((stages, count)),
            pltpu.SemaphoreType.DMA((stages, count)),
            pltpu.SemaphoreType.DMA((2, up_n)),
            pltpu.SemaphoreType.DMA((2, up_n)),
        ],
        compiler_params=pltpu.CompilerParams(
            collective_id=0, has_side_effects=True, vmem_limit_bytes=56 * 1024 * 1024
        ),
        cost_estimate=pl.CostEstimate(
            flops=2 * macs, bytes_accessed=32 * 1024 * 1024, transcendentals=0
        ),
        name="forward_products",
    )(cotangent, normed, *weights)


def scatter_kernel(
    depth,
    peers,
    partial,
    gain_ref,
    unit_ref,
    inverse_ref,
    grad_out,
    pair_send,
    pair_recv,
    up_send,
    up_recv,
    down_send,
    down_recv,
    sums,
    pair_sems,
    up_sems,
    down_sems,
    sum_sems,
):
    hid, wid = lax.axis_index("hid"), lax.axis_index("wid")
    z, y = hid // 2, hid % 2
    above, below, pair = hid + 2, hid - 2, z * 2 + 1 - y
    barrier = pltpu.get_barrier_semaphore()
    pl.semaphore_signal(barrier, inc=1, device_id={"hid": pair}, device_id_type=MESH)
    for turn in range(1, peers):
        pl.semaphore_signal(
            barrier, inc=1, device_id={"wid": (wid + turn) % peers}, device_id_type=MESH
        )

    @pl.when(z < depth - 1)
    def _():
        pl.semaphore_signal(barrier, inc=1, device_id={"hid": above}, device_id_type=MESH)

    @pl.when(z > 0)
    def _():
        pl.semaphore_signal(barrier, inc=1, device_id={"hid": below}, device_id_type=MESH)

    pl.semaphore_wait(barrier, peers + jnp.where(z > 0, 1, 0) + jnp.where(z < depth - 1, 1, 0))

    def block_copy(source, target, sems, level, device):
        return pltpu.make_async_remote_copy(
            src_ref=source.at[level],
            dst_ref=target.at[level],
            send_sem=sems.at[0, level],
            recv_sem=sems.at[1, level],
            device_id={"hid": device},
            device_id_type=MESH,
        )

    def pair_copy(level):
        return block_copy(pair_send, pair_recv, pair_sems, level, pair)

    def up_copy(level):
        return block_copy(up_send, up_recv, up_sems, level, above)

    def down_copy(level):
        return block_copy(down_send, down_recv, down_sems, level, below)

    def give(level):
        pair_send[level] = partial[level * 2 + 1 - y].astype(jnp.bfloat16)
        pair_copy(level).start()

    def joined(level):
        pair_copy(level).wait_recv()
        return partial[level * 2 + y] + pair_recv[level].astype(jnp.float32)

    for far in range(depth - 1, 0, -1):

        @pl.when(z + far <= depth - 1)
        def _():
            give(z + far)

        @pl.when(z - far >= 0)
        def _():
            give(z - far)

    give(z)

    for far in range(depth - 1, 0, -1):

        @pl.when(z + far <= depth - 1)
        def _():
            level = z + far
            held = joined(level)

            @pl.when(z > 0)
            def _():
                up_copy(level).wait_recv()
                up_send[level] = (held + up_recv[level].astype(jnp.float32)).astype(jnp.bfloat16)

            @pl.when(z == 0)
            def _():
                up_send[level] = held.astype(jnp.bfloat16)

            up_copy(level).start()

        @pl.when(z - far >= 0)
        def _():
            level = z - far
            held = joined(level)

            @pl.when(z < depth - 1)
            def _():
                down_copy(level).wait_recv()
                down_send[level] = (held + down_recv[level].astype(jnp.float32)).astype(
                    jnp.bfloat16
                )

            @pl.when(z == depth - 1)
            def _():
                down_send[level] = held.astype(jnp.bfloat16)

            down_copy(level).start()

    partial[hid] = joined(z)

    @pl.when(z > 0)
    def _():
        up_copy(z).wait_recv()
        partial[hid] = partial[hid] + up_recv[z].astype(jnp.float32)

    @pl.when(z < depth - 1)
    def _():
        down_copy(z).wait_recv()
        partial[hid] = partial[hid] + down_recv[z].astype(jnp.float32)

    unit_grad = partial[hid] * gain_ref[...]
    unit_rows = unit_ref[...]
    rows, columns = unit_rows.shape
    plain = jnp.sum(unit_grad, axis=-1, keepdims=True)
    project = jnp.sum(unit_grad * unit_rows, axis=-1, keepdims=True)
    lane = lax.broadcasted_iota(jnp.int32, (rows, 128), 1)
    sums[wid] = jnp.where(lane < 64, plain, project)

    def sum_copy(slot, turn):
        return pltpu.make_async_remote_copy(
            src_ref=sums.at[slot],
            dst_ref=sums.at[slot],
            send_sem=sum_sems.at[0, turn],
            recv_sem=sum_sems.at[1, slot],
            device_id={"wid": (wid + turn) % peers},
            device_id_type=MESH,
        )

    for turn in range(1, peers):
        sum_copy(wid, turn).start()
    for turn in range(1, peers):
        sum_copy((wid + turn) % peers, turn).wait_recv()
    joint = sums[0]
    for at in range(1, peers):
        joint = joint + sums[at]
    joint = joint * (1.0 / (columns * peers))
    grad_out[...] = (
        inverse_ref[...] * (unit_grad - joint[:, 0:1] - unit_rows * joint[:, 64:65])
    ).astype(jnp.bfloat16)

    for turn in range(1, peers):
        sum_copy(wid, turn).wait_send()
    for level in range(depth):
        pair_copy(level).wait_send()

        @pl.when(level > z)
        def _():
            up_copy(level).wait_send()

        @pl.when(level < z)
        def _():
            down_copy(level).wait_send()


def scatter_back(partial, norm_gain, unit_rows, inverse):
    size, peers = lax.axis_size("hid"), lax.axis_size("wid")
    depth = size // 2
    rows, columns = unit_rows.shape
    vmem = pl.BlockSpec(memory_space=pltpu.VMEM)

    def body(partial_in, gain_ref, unit_ref, inverse_ref, grad_out, partial_held, *rest):
        partial_held[...] = partial_in[...]
        scatter_kernel(
            depth, peers, partial_held, gain_ref, unit_ref, inverse_ref, grad_out, *rest
        )

    block = pltpu.VMEM((depth, rows, columns), jnp.bfloat16)
    pairs = pltpu.SemaphoreType.DMA((2, depth))
    return pl.pallas_call(
        body,
        out_shape=jax.ShapeDtypeStruct((rows, columns), jnp.bfloat16),
        in_specs=[vmem] * 4,
        out_specs=vmem,
        scratch_shapes=[pltpu.VMEM((size, rows, columns), jnp.float32)]
        + [block] * 6
        + [pltpu.VMEM((peers, rows, 128), jnp.float32)]
        + [pairs] * 3
        + [pltpu.SemaphoreType.DMA((2, peers))],
        compiler_params=pltpu.CompilerParams(
            collective_id=1, has_side_effects=True, vmem_limit_bytes=24 * 1024 * 1024
        ),
        cost_estimate=pl.CostEstimate(
            flops=16 * size * rows * columns,
            bytes_accessed=4 * size * rows * columns,
            transcendentals=0,
        ),
        name="scatter_back",
    )(
        partial.reshape(size, rows, columns),
        norm_gain.reshape(1, columns),
        unit_rows,
        inverse,
    )


def both_halves(own, core):
    other = swapped(own, "wid", 1)
    return jnp.concatenate(
        [jnp.where(core == 0, own, other), jnp.where(core == 0, other, own)], axis=0
    )


def local(
    inputs,
    cotangent,
    norm_gain,
    qkv_weight,
    out_weight,
    up_weight,
    down_weight,
    query_gain,
    key_gain,
):
    core = lax.axis_index("wid") % 2
    input_rows = inputs.astype(jnp.float32)
    centre, inverse = row_moments(input_rows)
    inverse = inverse[:, None]
    unit_rows = (input_rows - centre[:, None]) * inverse
    normed = (unit_rows * norm_gain).astype(jnp.bfloat16)
    grad_all, normed_all, att_grad, qkv_rows, hidden, pre_grad = forward_products(
        cotangent,
        normed,
        out_weight,
        down_weight,
        jnp.transpose(qkv_weight, (1, 0, 2)),
        up_weight,
    )
    grad_all = grad_all.reshape(-1, grad_all.shape[2])
    normed_all = normed_all.reshape(-1, normed_all.shape[2])
    attended, qkv_back = attention_pair(
        jnp.transpose(qkv_rows, (1, 0, 2)), att_grad, query_gain, key_gain
    )
    qkv_back = both_halves(qkv_back, core)
    attended = both_halves(attended, core)

    normed_grad = product("tf,df->td", pre_grad, up_weight) + product(
        "tch,dch->td", qkv_back, qkv_weight
    )
    up_grad = product("td,tf->df", normed_all, pre_grad).astype(jnp.bfloat16)
    down_grad = product("tf,td->fd", hidden, grad_all).astype(jnp.bfloat16)
    qkv_grad = product("td,tch->dch", normed_all, qkv_back).astype(jnp.bfloat16)
    out_grad = product("th,td->hd", attended, grad_all).astype(jnp.bfloat16)
    input_grad = scatter_back(normed_grad, norm_gain, unit_rows, inverse)
    return (input_grad, qkv_grad, out_grad, up_grad, down_grad)


def solution(mesh):
    placed = (
        P("hid", "wid"),
        P("hid", "wid"),
        P("wid"),
        P("wid", None, "hid"),
        P("hid", "wid"),
        P("wid", "hid"),
        P("hid", "wid"),
        P(),
        P(),
    )
    return jax.shard_map(
        local,
        mesh=mesh,
        in_specs=placed,
        out_specs=(
            P("hid", "wid"),
            P("wid", None, "hid"),
            P("hid", "wid"),
            P("wid", "hid"),
            P("hid", "wid"),
        ),
        check_vma=False,
    )
```

```python
import functools
import math

import jax
import jax.numpy as jnp
from jax import lax
from jax.experimental import pallas as pl
from jax.experimental.pallas import tpu as pltpu
from jax.sharding import PartitionSpec as P

HEAD_DIM = 128
PATCHES = 256


EPSILON = 1e-06


def swapped(value, axis, bit):
    size = lax.axis_size(axis)
    return lax.ppermute(value, axis, [(at, at ^ bit) for at in range(size)])


def product(form, left_arr, right_arr):
    return jnp.einsum(form, left_arr, right_arr, preferred_element_type=jnp.float32)


def head_norm(values, gain):
    centre = jnp.mean(values, axis=-1, keepdims=True)
    centred = values - centre
    inverse = lax.rsqrt(jnp.mean(centred * centred, axis=-1, keepdims=True) + EPSILON)
    unit_rows = centred * inverse
    return (unit_rows, inverse, unit_rows * gain)


def head_norm_back(upstream, unit_rows, inverse, gain):
    scaled = upstream * gain
    return inverse * (
        scaled
        - jnp.mean(scaled, axis=-1, keepdims=True)
        - unit_rows * jnp.mean(scaled * unit_rows, axis=-1, keepdims=True)
    )


def attention_pair(qkv_rows, att_grad, query_gain, key_gain):
    tok_count = qkv_rows.shape[0]
    head_width = qkv_rows.shape[2]
    head_count = head_width // HEAD_DIM
    image_count = tok_count // PATCHES
    score_scale = 1.0 / math.sqrt(HEAD_DIM)

    def per_image(values):
        return values.reshape(image_count, PATCHES, head_count, HEAD_DIM)

    query_unit, query_inverse, query_normed = head_norm(per_image(qkv_rows[:, 0]), query_gain)
    key_unit, key_inverse, key_normed = head_norm(per_image(qkv_rows[:, 1]), key_gain)
    query_normed = query_normed.astype(jnp.bfloat16)
    key_normed = key_normed.astype(jnp.bfloat16)
    value_rows = per_image(qkv_rows[:, 2]).astype(jnp.bfloat16)
    scores = product("ipha,iqha->ihpq", query_normed, key_normed) * score_scale
    exponent = jnp.exp(scores)
    probs = exponent / jnp.sum(exponent, axis=-1, keepdims=True)
    probs_low = probs.astype(jnp.bfloat16)
    attended = (
        product("ihpq,iqha->ipha", probs_low, value_rows)
        .astype(jnp.bfloat16)
        .reshape(tok_count, head_width)
    )
    grad_rows = per_image(att_grad)
    probs_grad = product("ipha,iqha->ihpq", grad_rows, value_rows)
    value_grad = product("ihpq,ipha->iqha", probs_low, grad_rows)
    score_grad = (
        probs * (probs_grad - jnp.sum(probs * probs_grad, axis=-1, keepdims=True)) * score_scale
    ).astype(jnp.bfloat16)
    qn_grad = product("ihpq,iqha->ipha", score_grad, key_normed)
    kn_grad = product("ihpq,ipha->iqha", score_grad, query_normed)
    query_grad = head_norm_back(qn_grad, query_unit, query_inverse, query_gain)
    key_grad = head_norm_back(kn_grad, key_unit, key_inverse, key_gain)
    qkv_back = jnp.stack(
        [
            query_grad.reshape(tok_count, head_width),
            key_grad.reshape(tok_count, head_width),
            value_grad.reshape(tok_count, head_width),
        ],
        axis=1,
    ).astype(jnp.bfloat16)
    return (attended, qkv_back)


MESH = pl.DeviceIdType.MESH
GELU_SLOPE = math.sqrt(2.0 / math.pi)
GELU_CUBE = 0.044715


def gelu_both(pre_act, upstream):
    square = pre_act * pre_act
    bend = jnp.tanh(GELU_SLOPE * pre_act * (1.0 + GELU_CUBE * square))
    lift = 0.5 * (1.0 + bend)
    slope = GELU_SLOPE * (1.0 + 3.0 * GELU_CUBE * square)
    derivative = lift + 0.5 * pre_act * (1.0 - bend * bend) * slope
    return (pre_act * lift, derivative * upstream)


CHUNK = 512


def forward_kernel(
    sizes,
    cot_ref,
    inputs_ref,
    gain_ref,
    out_ref,
    down_ref,
    qkv_ref,
    up_ref,
    cot_all,
    normed_all,
    att_out,
    qkv_out,
    hidden_all,
    pre_all,
    unit_out,
    inverse_out,
    total,
    out_w,
    down_w,
    qkv_w,
    up_w,
    core_send,
    core_recv,
    x_send,
    x_recv,
    load_sem,
    slot_sem,
    rise_sem,
    fall_sem,
    pair_sem,
    core_out_sem,
    core_in_sem,
    x_out_sem,
    x_in_sem,
    hand_out_sem,
    hand_in_sem,
    moments,
    moment_sems,
):
    depth, out_n, down_n, up_n, width, stages = sizes
    hid, wid = lax.axis_index("hid"), lax.axis_index("wid")
    z, y = hid // 2, hid % 2
    core = wid % 2
    above, below, pair = hid + 2, hid - 2, z * 2 + 1 - y
    core_peer = wid + 1 - 2 * core
    x_peers = [
        wid + bit - 2 * bit * ((wid // bit) % 2) for bit in (2 << at for at in range(stages))
    ]

    loads = [
        pltpu.make_async_copy(src, dst, load_sem.at[at])
        for at, (src, dst) in enumerate(
            [(out_ref, out_w), (down_ref, down_w), (qkv_ref, qkv_w), (up_ref, up_w)]
        )
    ]
    for load in loads:
        load.start()

    gathered = (cot_all, normed_all)
    cot_all[hid] = cot_ref[...]
    peers = moments.shape[0]

    barrier = pltpu.get_barrier_semaphore()
    pl.semaphore_signal(barrier, inc=1, device_id={"hid": pair}, device_id_type=MESH)
    for turn in range(1, peers):
        pl.semaphore_signal(
            barrier, inc=1, device_id={"wid": (wid + turn) % peers}, device_id_type=MESH
        )

    @pl.when(z < depth - 1)
    def _():
        pl.semaphore_signal(barrier, inc=1, device_id={"hid": above}, device_id_type=MESH)

    @pl.when(z > 0)
    def _():
        pl.semaphore_signal(barrier, inc=1, device_id={"hid": below}, device_id_type=MESH)

    neighbours = peers + jnp.where(z > 0, 1, 0) + jnp.where(z < depth - 1, 1, 0)
    pl.semaphore_wait(barrier, neighbours)

    def block_copy(kind, level, side, sems, target):
        slot = level * 2 + side
        return pltpu.make_async_remote_copy(
            src_ref=gathered[kind].at[slot],
            dst_ref=gathered[kind].at[slot],
            send_sem=sems.at[kind, level],
            recv_sem=slot_sem.at[kind, slot],
            device_id={"hid": target},
            device_id_type=MESH,
        )

    def to_pair(kind, level):
        return block_copy(kind, level, y, pair_sem, pair)

    def upward(kind, level):
        return block_copy(kind, level, y, rise_sem, above)

    def downward(kind, level):
        return block_copy(kind, level, y, fall_sem, below)

    def begin(kind):
        @pl.when(z < depth - 1)
        def _():
            upward(kind, z).start()

        @pl.when(z > 0)
        def _():
            downward(kind, z).start()

        to_pair(kind, z).start()

    def relay(kind, step):
        @pl.when(z - step >= 0)
        def _():
            level = z - step
            upward(kind, level).wait_recv()

            @pl.when(z < depth - 1)
            def _():
                upward(kind, level).start()

            to_pair(kind, level).start()

        @pl.when(z + step <= depth - 1)
        def _():
            level = z + step
            downward(kind, level).wait_recv()

            @pl.when(z > 0)
            def _():
                downward(kind, level).start()

            to_pair(kind, level).start()

    def pair_arrived(kind, image):
        for at in range(depth // 2):
            block_copy(kind, image * (depth // 2) + at, 1 - y, pair_sem, pair).wait_recv()

    def core_copy(at):
        return pltpu.make_async_remote_copy(
            src_ref=core_send.at[at],
            dst_ref=core_recv.at[at],
            send_sem=core_out_sem.at[at],
            recv_sem=core_in_sem.at[at],
            device_id={"wid": core_peer},
            device_id_type=MESH,
        )

    def x_copy(at, stage=0):
        return pltpu.make_async_remote_copy(
            src_ref=x_send.at[stage, at],
            dst_ref=x_recv.at[stage, at],
            send_sem=x_out_sem.at[stage, at],
            recv_sem=x_in_sem.at[stage, at],
            device_id={"wid": x_peers[stage]},
            device_id_type=MESH,
        )

    def combine(at):
        core_copy(at).wait_recv()
        subtotal = total[at] + core_recv[at].astype(jnp.float32)
        total[at] = subtotal
        x_send[0, at] = subtotal.astype(jnp.bfloat16)
        x_copy(at).start()

    def place(image, at, part):
        @pl.when(image == core)
        def _():
            total[at] = part

            @pl.when(at > 0)
            def _():
                combine(at - 1)

        @pl.when(image != core)
        def _():
            core_send[at] = part.astype(jnp.bfloat16)
            core_copy(at).start()

    def rows_of(kind, image):
        rows = gathered[kind][pl.ds(image * depth, depth)]
        return rows.reshape(rows.shape[0] * rows.shape[1], rows.shape[2])

    def turned(rows, weight):
        return lax.dot_general(
            rows, weight, (((1,), (1,)), ((), ())), preferred_element_type=jnp.float32
        )

    def straight(rows, weight):
        return jnp.dot(rows, weight, preferred_element_type=jnp.float32)

    def span(at):
        return pl.ds(pl.multiple_of(at * width, width), width)

    first_qkv = out_n + down_n
    first_up = first_qkv + 3

    def cot_products(image):
        @pl.loop(0, out_n)
        def _(at):
            place(image, at, turned(rows_of(0, image), out_w[span(at), :]))

        @pl.loop(0, down_n)
        def _(at):
            place(image, out_n + at, turned(rows_of(0, image), down_w[span(at), :]))

    def qkv_products(image):
        @pl.loop(0, 3)
        def _(at):
            place(image, first_qkv + at, straight(rows_of(1, image), qkv_w[at]))

    def up_products(image):
        @pl.loop(0, up_n)
        def _(at):
            place(image, first_up + at, straight(rows_of(1, image), up_w[:, span(at)]))

        @pl.when(image == core)
        def _():
            combine(first_up + up_n - 1)

    def hand_copy(kind, at, image):
        block = ((hidden_all, pre_all)[kind]).at[image_rows(image), span(at)]
        return pltpu.make_async_remote_copy(
            src_ref=block,
            dst_ref=block,
            send_sem=hand_out_sem.at[kind, at],
            recv_sem=hand_in_sem.at[kind, at],
            device_id={"wid": core_peer},
            device_id_type=MESH,
        )

    def image_rows(image):
        half = total.shape[1]
        return pl.ds(pl.multiple_of(image * half, half), half)

    def moment_copy(slot, turn):
        return pltpu.make_async_remote_copy(
            src_ref=moments.at[slot],
            dst_ref=moments.at[slot],
            send_sem=moment_sems.at[0, turn],
            recv_sem=moment_sems.at[1, slot],
            device_id={"wid": (wid + turn) % peers},
            device_id_type=MESH,
        )

    begin(0)
    values = inputs_ref[...].astype(jnp.float32)
    rows, columns = values.shape
    mean = jnp.mean(values, axis=-1, keepdims=True)
    deviation = values - mean
    square = jnp.sum(deviation * deviation, axis=-1, keepdims=True)
    lane = lax.broadcasted_iota(jnp.int32, (rows, 128), 1)
    moments[wid] = jnp.where(lane < 64, mean, square)
    for turn in range(1, peers):
        moment_copy(wid, turn).start()
    for turn in range(1, peers):
        moment_copy((wid + turn) % peers, turn).wait_recv()
    shares = [moments[at] for at in range(peers)]
    centre = sum(share[:, 0:1] for share in shares) * (1.0 / peers)
    spread = sum(
        share[:, 64:65] + columns * (share[:, 0:1] - centre) * (share[:, 0:1] - centre)
        for share in shares
    )
    inverse = lax.rsqrt(spread * (1.0 / (columns * peers)) + EPSILON)
    unit_rows = (values - centre) * inverse
    unit_out[...] = unit_rows
    inverse_out[...] = jnp.broadcast_to(inverse, (rows, 128))
    normed_all[hid] = (unit_rows * gain_ref[...]).astype(jnp.bfloat16)
    begin(1)
    near = z // (depth // 2)
    far = 1 - near
    for step in range(1, depth // 2):
        relay(0, step)
        relay(1, step)
    late = list(range(depth // 2, depth))
    pair_arrived(0, near)
    for load in loads[:2]:
        load.wait()
    cot_products(near)
    for step in late[: len(late) // 2]:
        relay(0, step)
        relay(1, step)
    pair_arrived(1, near)
    for load in loads[2:]:
        load.wait()
    qkv_products(near)
    for step in late[len(late) // 2 :]:
        relay(0, step)
        relay(1, step)
    up_products(near)
    pair_arrived(0, far)
    cot_products(far)
    pair_arrived(1, far)
    qkv_products(far)
    up_products(far)

    def arrived(at, stage):
        x_copy(at, stage).wait_recv()
        return total[at] + x_recv[stage, at].astype(jnp.float32)

    for stage in range(stages - 1):

        @pl.loop(0, first_up + up_n)
        def _(at):
            subtotal = arrived(at, stage)
            total[at] = subtotal
            x_send[stage + 1, at] = subtotal.astype(jnp.bfloat16)
            x_copy(at, stage + 1).start()

    last = stages - 1
    for at in range(out_n):
        att_out[:, at * width : (at + 1) * width] = arrived(at, last).astype(jnp.bfloat16)

    @pl.loop(0, down_n)
    def _(at):
        total[out_n + at] = arrived(out_n + at, last)

    @pl.loop(0, 3)
    def _(at):
        qkv_out[at] = arrived(first_qkv + at, last)

    @pl.loop(0, up_n)
    def _(at):
        hidden, pre_grad = gelu_both(arrived(first_up + at, last), total[out_n + at])
        hidden_all[image_rows(core), span(at)] = hidden.astype(jnp.bfloat16)
        pre_all[image_rows(core), span(at)] = pre_grad.astype(jnp.bfloat16)
        hand_copy(1, at, core).start()
        hand_copy(0, at, core).start()

    @pl.loop(0, up_n)
    def _(at):
        hand_copy(1, at, 1 - core).wait_recv()
        hand_copy(0, at, 1 - core).wait_recv()
        hand_copy(1, at, core).wait_send()
        hand_copy(0, at, core).wait_send()

    @pl.loop(0, first_up + up_n)
    def _(at):
        core_copy(at).wait_send()
        for stage in range(stages):
            x_copy(at, stage).wait_send()

    for turn in range(1, peers):
        moment_copy(wid, turn).wait_send()
    for kind in range(2):
        for level in range(depth):
            to_pair(kind, level).wait_send()

            @pl.when((z < depth - 1) & (level <= z))
            def _():
                upward(kind, level).wait_send()

            @pl.when((z > 0) & (level >= z))
            def _():
                downward(kind, level).wait_send()


def forward_products(
    cotangent, inputs, norm_gain, out_weight, down_weight, qkv_weight, up_weight
):
    blocks = lax.axis_size("hid")
    depth = blocks // 2
    rows, columns = cotangent.shape
    width = min(CHUNK, out_weight.shape[0])
    out_n, down_n, up_n = (
        out_weight.shape[0] // width,
        down_weight.shape[0] // width,
        up_weight.shape[1] // width,
    )
    assert qkv_weight.shape[2] == width
    count = out_n + down_n + 3 + up_n
    half = rows * depth
    stages = lax.axis_size("wid").bit_length() - 2
    vmem = pl.BlockSpec(memory_space=pltpu.VMEM)
    hbm = pl.BlockSpec(memory_space=pl.ANY)
    all_shape = jax.ShapeDtypeStruct((blocks, rows, columns), jnp.bfloat16)
    weights = (out_weight, down_weight, qkv_weight, up_weight)
    slots = pltpu.VMEM((count, half, width), jnp.bfloat16)
    macs = 2 * half * columns * width * count
    return pl.pallas_call(
        functools.partial(forward_kernel, (depth, out_n, down_n, up_n, width, stages)),
        out_shape=(
            all_shape,
            all_shape,
            jax.ShapeDtypeStruct((half, out_weight.shape[0]), jnp.bfloat16),
            jax.ShapeDtypeStruct((3, half, width), jnp.float32),
            jax.ShapeDtypeStruct((2 * half, up_weight.shape[1]), jnp.bfloat16),
            jax.ShapeDtypeStruct((2 * half, up_weight.shape[1]), jnp.bfloat16),
            jax.ShapeDtypeStruct((rows, columns), jnp.float32),
            jax.ShapeDtypeStruct((rows, 128), jnp.float32),
        ),
        in_specs=[vmem, vmem, vmem, hbm, hbm, hbm, hbm],
        out_specs=(vmem,) * 8,
        scratch_shapes=[pltpu.VMEM((count, half, width), jnp.float32)]
        + [pltpu.VMEM(weight.shape, weight.dtype) for weight in weights]
        + [slots] * 2
        + [pltpu.VMEM((stages, count, half, width), jnp.bfloat16)] * 2
        + [
            pltpu.SemaphoreType.DMA((4,)),
            pltpu.SemaphoreType.DMA((2, blocks)),
            pltpu.SemaphoreType.DMA((2, depth)),
            pltpu.SemaphoreType.DMA((2, depth)),
            pltpu.SemaphoreType.DMA((2, depth)),
            pltpu.SemaphoreType.DMA((count,)),
            pltpu.SemaphoreType.DMA((count,)),
            pltpu.SemaphoreType.DMA((stages, count)),
            pltpu.SemaphoreType.DMA((stages, count)),
            pltpu.SemaphoreType.DMA((2, up_n)),
            pltpu.SemaphoreType.DMA((2, up_n)),
            pltpu.VMEM((2 << stages, rows, 128), jnp.float32),
            pltpu.SemaphoreType.DMA((2, 2 << stages)),
        ],
        compiler_params=pltpu.CompilerParams(
            collective_id=0, has_side_effects=True, vmem_limit_bytes=56 * 1024 * 1024
        ),
        cost_estimate=pl.CostEstimate(
            flops=2 * macs, bytes_accessed=32 * 1024 * 1024, transcendentals=0
        ),
        name="forward_products",
    )(cotangent, inputs, norm_gain.reshape(1, columns), *weights)


def scatter_kernel(
    depth,
    peers,
    partial,
    gain_ref,
    unit_ref,
    inverse_ref,
    grad_out,
    pair_send,
    pair_recv,
    up_send,
    up_recv,
    down_send,
    down_recv,
    sums,
    pair_sems,
    up_sems,
    down_sems,
    sum_sems,
):
    hid, wid = lax.axis_index("hid"), lax.axis_index("wid")
    z, y = hid // 2, hid % 2
    above, below, pair = hid + 2, hid - 2, z * 2 + 1 - y
    barrier = pltpu.get_barrier_semaphore()
    pl.semaphore_signal(barrier, inc=1, device_id={"hid": pair}, device_id_type=MESH)
    for turn in range(1, peers):
        pl.semaphore_signal(
            barrier, inc=1, device_id={"wid": (wid + turn) % peers}, device_id_type=MESH
        )

    @pl.when(z < depth - 1)
    def _():
        pl.semaphore_signal(barrier, inc=1, device_id={"hid": above}, device_id_type=MESH)

    @pl.when(z > 0)
    def _():
        pl.semaphore_signal(barrier, inc=1, device_id={"hid": below}, device_id_type=MESH)

    pl.semaphore_wait(barrier, peers + jnp.where(z > 0, 1, 0) + jnp.where(z < depth - 1, 1, 0))

    def block_copy(source, target, sems, level, device):
        return pltpu.make_async_remote_copy(
            src_ref=source.at[level],
            dst_ref=target.at[level],
            send_sem=sems.at[0, level],
            recv_sem=sems.at[1, level],
            device_id={"hid": device},
            device_id_type=MESH,
        )

    def pair_copy(level):
        return block_copy(pair_send, pair_recv, pair_sems, level, pair)

    def up_copy(level):
        return block_copy(up_send, up_recv, up_sems, level, above)

    def down_copy(level):
        return block_copy(down_send, down_recv, down_sems, level, below)

    def give(level):
        pair_send[level] = partial[level * 2 + 1 - y].astype(jnp.bfloat16)
        pair_copy(level).start()

    def joined(level):
        pair_copy(level).wait_recv()
        return partial[level * 2 + y] + pair_recv[level].astype(jnp.float32)

    for far in range(depth - 1, 0, -1):

        @pl.when(z + far <= depth - 1)
        def _():
            give(z + far)

        @pl.when(z - far >= 0)
        def _():
            give(z - far)

    give(z)

    for far in range(depth - 1, 0, -1):

        @pl.when(z + far <= depth - 1)
        def _():
            level = z + far
            held = joined(level)

            @pl.when(z > 0)
            def _():
                up_copy(level).wait_recv()
                up_send[level] = (held + up_recv[level].astype(jnp.float32)).astype(jnp.bfloat16)

            @pl.when(z == 0)
            def _():
                up_send[level] = held.astype(jnp.bfloat16)

            up_copy(level).start()

        @pl.when(z - far >= 0)
        def _():
            level = z - far
            held = joined(level)

            @pl.when(z < depth - 1)
            def _():
                down_copy(level).wait_recv()
                down_send[level] = (held + down_recv[level].astype(jnp.float32)).astype(
                    jnp.bfloat16
                )

            @pl.when(z == depth - 1)
            def _():
                down_send[level] = held.astype(jnp.bfloat16)

            down_copy(level).start()

    partial[hid] = joined(z)

    @pl.when(z > 0)
    def _():
        up_copy(z).wait_recv()
        partial[hid] = partial[hid] + up_recv[z].astype(jnp.float32)

    @pl.when(z < depth - 1)
    def _():
        down_copy(z).wait_recv()
        partial[hid] = partial[hid] + down_recv[z].astype(jnp.float32)

    unit_grad = partial[hid] * gain_ref[...]
    unit_rows = unit_ref[...]
    rows, columns = unit_rows.shape
    plain = jnp.sum(unit_grad, axis=-1, keepdims=True)
    project = jnp.sum(unit_grad * unit_rows, axis=-1, keepdims=True)
    lane = lax.broadcasted_iota(jnp.int32, (rows, 128), 1)
    sums[wid] = jnp.where(lane < 64, plain, project)

    def sum_copy(slot, turn):
        return pltpu.make_async_remote_copy(
            src_ref=sums.at[slot],
            dst_ref=sums.at[slot],
            send_sem=sum_sems.at[0, turn],
            recv_sem=sum_sems.at[1, slot],
            device_id={"wid": (wid + turn) % peers},
            device_id_type=MESH,
        )

    for turn in range(1, peers):
        sum_copy(wid, turn).start()
    for turn in range(1, peers):
        sum_copy((wid + turn) % peers, turn).wait_recv()
    joint = sums[0]
    for at in range(1, peers):
        joint = joint + sums[at]
    joint = joint * (1.0 / (columns * peers))
    grad_out[...] = (
        inverse_ref[:, 0:1] * (unit_grad - joint[:, 0:1] - unit_rows * joint[:, 64:65])
    ).astype(jnp.bfloat16)

    for turn in range(1, peers):
        sum_copy(wid, turn).wait_send()
    for level in range(depth):
        pair_copy(level).wait_send()

        @pl.when(level > z)
        def _():
            up_copy(level).wait_send()

        @pl.when(level < z)
        def _():
            down_copy(level).wait_send()


def scatter_back(partial, norm_gain, unit_rows, inverse):
    size, peers = lax.axis_size("hid"), lax.axis_size("wid")
    depth = size // 2
    rows, columns = unit_rows.shape
    vmem = pl.BlockSpec(memory_space=pltpu.VMEM)

    def body(partial_in, gain_ref, unit_ref, inverse_ref, grad_out, partial_held, *rest):
        partial_held[...] = partial_in[...]
        scatter_kernel(
            depth, peers, partial_held, gain_ref, unit_ref, inverse_ref, grad_out, *rest
        )

    block = pltpu.VMEM((depth, rows, columns), jnp.bfloat16)
    pairs = pltpu.SemaphoreType.DMA((2, depth))
    return pl.pallas_call(
        body,
        out_shape=jax.ShapeDtypeStruct((rows, columns), jnp.bfloat16),
        in_specs=[vmem] * 4,
        out_specs=vmem,
        scratch_shapes=[pltpu.VMEM((size, rows, columns), jnp.float32)]
        + [block] * 6
        + [pltpu.VMEM((peers, rows, 128), jnp.float32)]
        + [pairs] * 3
        + [pltpu.SemaphoreType.DMA((2, peers))],
        compiler_params=pltpu.CompilerParams(
            collective_id=1, has_side_effects=True, vmem_limit_bytes=24 * 1024 * 1024
        ),
        cost_estimate=pl.CostEstimate(
            flops=16 * size * rows * columns,
            bytes_accessed=4 * size * rows * columns,
            transcendentals=0,
        ),
        name="scatter_back",
    )(
        partial.reshape(size, rows, columns),
        norm_gain.reshape(1, columns),
        unit_rows,
        inverse,
    )


def both_halves(own, core):
    other = swapped(own, "wid", 1)
    return jnp.concatenate(
        [jnp.where(core == 0, own, other), jnp.where(core == 0, other, own)], axis=0
    )


def local(
    inputs,
    cotangent,
    norm_gain,
    qkv_weight,
    out_weight,
    up_weight,
    down_weight,
    query_gain,
    key_gain,
):
    core = lax.axis_index("wid") % 2
    (
        grad_all,
        normed_all,
        att_grad,
        qkv_rows,
        hidden,
        pre_grad,
        unit_rows,
        inverse,
    ) = forward_products(
        cotangent,
        inputs,
        norm_gain,
        out_weight,
        down_weight,
        jnp.transpose(qkv_weight, (1, 0, 2)),
        up_weight,
    )
    grad_all = grad_all.reshape(-1, grad_all.shape[2])
    normed_all = normed_all.reshape(-1, normed_all.shape[2])
    attended, qkv_back = attention_pair(
        jnp.transpose(qkv_rows, (1, 0, 2)), att_grad, query_gain, key_gain
    )
    qkv_back = both_halves(qkv_back, core)
    attended = both_halves(attended, core)

    normed_grad = product("tf,df->td", pre_grad, up_weight) + product(
        "tch,dch->td", qkv_back, qkv_weight
    )
    up_grad = product("td,tf->df", normed_all, pre_grad).astype(jnp.bfloat16)
    down_grad = product("tf,td->fd", hidden, grad_all).astype(jnp.bfloat16)
    qkv_grad = product("td,tch->dch", normed_all, qkv_back).astype(jnp.bfloat16)
    out_grad = product("th,td->hd", attended, grad_all).astype(jnp.bfloat16)
    input_grad = scatter_back(normed_grad, norm_gain, unit_rows, inverse)
    return (input_grad, qkv_grad, out_grad, up_grad, down_grad)


def solution(mesh):
    placed = (
        P("hid", "wid"),
        P("hid", "wid"),
        P("wid"),
        P("wid", None, "hid"),
        P("hid", "wid"),
        P("wid", "hid"),
        P("hid", "wid"),
        P(),
        P(),
    )
    return jax.shard_map(
        local,
        mesh=mesh,
        in_specs=placed,
        out_specs=(
            P("hid", "wid"),
            P("wid", None, "hid"),
            P("hid", "wid"),
            P("wid", "hid"),
            P("hid", "wid"),
        ),
        check_vma=False,
    )
```
